512 devices in a mesh: dp: 16 (over y, core), expert: 32 (over x, z).
Axes of the slice: x: 4, y: 8, z: 8, core: 2. Of those that a mesh axis runs over, the one named last changes fastest.
Arguments:
- tokens: bfloat16 [65536, 1024], P(('dp', 'expert')), may hold values from -6 to 6
- cotangent: bfloat16 [65536, 1024], P(('dp', 'expert')), may hold values from -24 to 24
- router_weight: float32 [32, 1024], replicated, may hold values from -0.1875 to 0.1875
- gate_weight: bfloat16 [32, 1024, 768], P('expert', 'dp'), may hold values from -0.1875 to 0.1875
- up_weight: bfloat16 [32, 1024, 768], P('expert', 'dp'), may hold values from -0.1875 to 0.1875
- down_weight: bfloat16 [32, 768, 1024], P('expert', 'dp'), may hold values from -0.21875 to 0.21875
- routes: int32 [65536, 6], P(('dp', 'expert')), may hold values from 0 to 31, all different within a row
- drop_mask: int32 [65536], P(('dp', 'expert')), may hold values 0 or 1
Outputs:
- token_grad: bfloat16 [65536, 1024], P(('dp', 'expert'))
- gate_grad: bfloat16 [32, 1024, 768], P('expert', 'dp')
- up_grad: bfloat16 [32, 1024, 768], P('expert', 'dp')
- router_grad: float32 [32, 1024], replicated
The draws below stay inside these ranges and needn't reach their ends.
Inputs may be any that keep to these rules, and one draw needn't show every extreme that they name: `routes`: each row names 6 different experts, and every expert is named by some row.
All inputs are finite; a program needn't handle non-finite values. No bound on the sum of `drop_mask` on one device may be relied on, other than what follows from the above.
Results may differ from the reference program's by a relative error of at most 0.023.
Values may be sent and summed in bfloat16 or wider, within the bound.
No kernel may reach another device: no remote copies, remote signals or barrier semaphores. Data moves between devices by JAX's collectives and lax.ppermute only.
A program may use at most 64 MiB of HBM per device.

```python
from functools import partial
import jax
import jax.numpy as jnp
from jax import lax

D = 1024
HID = 768
TOPK = 6
TOK_DEV = 128
EXPERTS = 32
TOKENS = 65536
CAP = 16
N_DP = 16
N_EXPERT = 32


def touch_ends(entries, rng, smallest, top_value):
    extent = entries.shape
    spot = [jax.random.randint(jax.random.fold_in(rng, axis), (), 0, extent[axis]) for axis in range(len(extent))]
    entries = entries.at[tuple(spot)].set(smallest)
    longest = extent.index(max(extent))
    spot[longest] = (spot[longest] + 1) % extent[longest]
    return entries.at[tuple(spot)].set(top_value)


def levels(own_key, dims, pieces, smallest, high):
    def one(position, blocks):
        steps = jax.random.uniform(jax.random.fold_in(jax.random.fold_in(own_key, 6), position), (blocks,), jnp.float32, smallest / len(pieces), high / len(pieces))
        return jnp.repeat(jnp.exp(steps), dims[position] // blocks).reshape((-1,) + (1,) * (len(dims) - position - 1))

    loudness = one(*pieces[0])
    for cut in pieces[1:]:
        loudness = loudness * one(*cut)
    return loudness


def distinct(stream_key, rows, count, top, lift):
    order = jax.random.permutation(jax.random.fold_in(stream_key, 1), count)
    pull = order
    for power in range(3):
        pull = pull * pull // count
    pull = pull * lift // count
    chance = jax.random.randint(jax.random.fold_in(stream_key, 2), (rows, count), 0, 4096) + pull
    fixed_rows = jax.random.permutation(jax.random.fold_in(stream_key, 3), rows)[jnp.arange(count) % rows]
    chance = jnp.where(jnp.arange(rows)[:, None] == fixed_rows[None, :], 1 << 14, chance)
    priority = chance * count + jnp.arange(count)
    return lax.top_k(priority.astype(jnp.int32), top)[1].astype(jnp.int32)


def scatter_about(key, shape, spread, bound, pieces=(), held_as=jnp.bfloat16):
    entries = jax.random.normal(key, shape, jnp.float32) * spread
    if len(pieces) > 0:
        entries = levels(key, shape, pieces, -0.22, 0.18) * entries
    return jnp.clip(entries, min=-bound, max=bound).astype(held_as)


def setup_inputs(seed: int = 0) -> dict:
    key_list = jax.random.split(jax.random.key(seed), 9)
    tokens = scatter_about(key_list[0], (TOKENS, D), 1.0, 6.0, ((0, 512),))
    cotangent = scatter_about(key_list[1], (TOKENS, D), 4.0, 24.0, ((0, 512),))
    router_weight = scatter_about(key_list[2], (EXPERTS, D), D ** -0.5, 0.1875, (), jnp.float32)
    gate_weight = scatter_about(key_list[3], (EXPERTS, D, HID), D ** -0.5, 0.1875, ((0, 32), (1, 16)))
    up_weight = scatter_about(key_list[4], (EXPERTS, D, HID), D ** -0.5, 0.1875, ((0, 32), (1, 16)))
    down_weight = scatter_about(key_list[5], (EXPERTS, HID, D), HID ** -0.5, 0.21875, ((0, 32), (1, 16)))
    routes = distinct(key_list[6], TOKENS, EXPERTS, TOPK, 1536)
    drop_mask = touch_ends((jax.random.randint(key_list[7], (TOKENS,), 0, 16) < 15).astype(jnp.int32), jax.random.fold_in(key_list[7], 1), 0, 1)
    return dict(tokens=tokens, cotangent=cotangent, router_weight=router_weight, gate_weight=gate_weight, up_weight=up_weight, down_weight=down_weight, routes=routes, drop_mask=drop_mask)


highest = lax.Precision.HIGHEST


def route_positions(block_routes, block_mask, experts, capacity):
    top_count = block_routes.shape[1]
    flat_routes = block_routes.reshape(-1).astype(jnp.int32)
    live_route = jnp.repeat(block_mask, top_count) == 1
    expert_ids = jnp.arange(experts, dtype=jnp.int32)
    matches = ((flat_routes[:, None] == expert_ids[None, :]) & live_route[:, None]).astype(jnp.int32)
    before = (jnp.cumsum(matches, axis=0) - matches).astype(jnp.int32)
    slot_index = jnp.sum(before * matches, axis=1).astype(jnp.int32)
    kept_route = live_route & (slot_index < capacity)
    sink_index = experts * capacity
    return jnp.where(kept_route, flat_routes * capacity + slot_index, sink_index).astype(jnp.int32)


def slot_sources(positions, experts, capacity):
    route_count = positions.shape[0]
    slot_table = jnp.full((experts * capacity + 1,), route_count, jnp.int32)
    slot_table = slot_table.at[positions].set(jnp.arange(route_count, dtype=jnp.int32))
    return slot_table[:experts * capacity]


def pack_block(block_tokens, block_cotangent, block_probs, positions, experts, capacity):
    top_count = block_probs.shape[1]
    features = block_tokens.shape[1]
    sources = slot_sources(positions, experts, capacity)
    token_index = (sources // top_count).astype(jnp.int32)
    token_pad = jnp.concatenate([block_tokens, jnp.zeros((1, features), block_tokens.dtype)], 0)
    cotan_pad = jnp.concatenate([block_cotangent, jnp.zeros((1, features), block_cotangent.dtype)], 0)
    prob_pad = jnp.concatenate([block_probs.reshape(-1), jnp.zeros((1,), block_probs.dtype)])
    return token_pad[token_index], cotan_pad[token_index], prob_pad[sources]


def unpack_block(grad_back, prob_back, positions, top_count):
    features = grad_back.shape[1]
    grad_pad = jnp.concatenate([grad_back, jnp.zeros((1, features), grad_back.dtype)], 0)
    prob_pad = jnp.concatenate([prob_back, jnp.zeros((1,), prob_back.dtype)])
    picked = grad_pad[positions].astype(jnp.float32)
    expert_sum = jnp.sum(picked.reshape(-1, top_count, features), axis=1)
    prob_route = prob_pad[positions].astype(jnp.float32).reshape(-1, top_count)
    return expert_sum, prob_route


def expert_grads(operands):
    slot_tokens, slot_cotangent, slot_probs, gate_w, up_w, down_w = operands
    gate_proj = jnp.dot(slot_tokens, gate_w, preferred_element_type=jnp.float32)
    up_proj = jnp.dot(slot_tokens, up_w, preferred_element_type=jnp.float32)
    sigmoid_gate = jax.nn.sigmoid(gate_proj)
    activated = gate_proj * sigmoid_gate
    slope = sigmoid_gate * (1.0 + gate_proj * (1.0 - sigmoid_gate))
    hidden_grad = jnp.dot(slot_cotangent, down_w.T, preferred_element_type=jnp.float32)
    prob_grad = jnp.sum(hidden_grad * activated * up_proj, axis=1).astype(jnp.bfloat16)
    scaled = slot_probs.astype(jnp.float32)[:, None] * hidden_grad
    gate_delta = (scaled * up_proj * slope).astype(jnp.bfloat16)
    up_delta = (scaled * activated).astype(jnp.bfloat16)
    slot_grad = (jnp.dot(gate_delta, gate_w.T, preferred_element_type=jnp.float32)
                 + jnp.dot(up_delta, up_w.T, preferred_element_type=jnp.float32)).astype(jnp.bfloat16)
    gate_part = jnp.dot(slot_tokens.T, gate_delta, preferred_element_type=jnp.float32).astype(jnp.bfloat16)
    up_part = jnp.dot(slot_tokens.T, up_delta, preferred_element_type=jnp.float32).astype(jnp.bfloat16)
    return slot_grad, prob_grad, gate_part, up_part


def to_experts(values, group_size, experts, capacity):
    trailing = values.shape[2:]
    values = values.reshape((group_size, experts, capacity) + trailing)
    values = jnp.moveaxis(values, 1, 0)
    return values.reshape((experts, group_size * capacity) + trailing)


def to_sources(values, group_size, experts, capacity):
    trailing = values.shape[2:]
    values = values.reshape((experts, group_size, capacity) + trailing)
    values = jnp.moveaxis(values, 1, 0)
    return values.reshape((group_size, experts * capacity) + trailing)


def reference(tokens, cotangent, router_weight, gate_weight, up_weight, down_weight, routes, drop_mask):
    group_size = N_EXPERT
    group_count = N_DP
    blocks = group_count * group_size
    logits = jnp.dot(tokens.astype(jnp.float32), router_weight.T, precision=highest)
    weights = jnp.exp(logits)
    router_probs = weights / jnp.sum(weights, axis=1, keepdims=True)
    route_probs = jnp.take_along_axis(router_probs, routes, axis=1).astype(jnp.bfloat16)
    route_probs = lax.optimization_barrier(route_probs)
    locate = partial(route_positions, experts=EXPERTS, capacity=CAP)
    positions = jax.vmap(locate)(routes.reshape(blocks, TOK_DEV, TOPK), drop_mask.reshape(blocks, TOK_DEV))

    group_tokens = tokens.reshape(group_count, group_size, TOK_DEV, D)
    group_cotangent = cotangent.reshape(group_count, group_size, TOK_DEV, D)
    group_probs = route_probs.reshape(group_count, group_size, TOK_DEV, TOPK)
    group_positions = positions.reshape(group_count, group_size, TOK_DEV * TOPK)
    packer = partial(pack_block, experts=EXPERTS, capacity=CAP)
    unpacker = partial(unpack_block, top_count=TOPK)

    def one_group(totals, inputs):
        block_tokens, block_cotangent, block_probs, block_positions = inputs
        sent_tokens, sent_cotangent, sent_probs = jax.vmap(packer)(block_tokens, block_cotangent, block_probs, block_positions)
        slot_tokens = to_experts(sent_tokens, group_size, EXPERTS, CAP)
        slot_cotangent = to_experts(sent_cotangent, group_size, EXPERTS, CAP)
        slot_probs = to_experts(sent_probs, group_size, EXPERTS, CAP)
        slot_grad, prob_grad, gate_part, up_part = lax.map(
            expert_grads, (slot_tokens, slot_cotangent, slot_probs, gate_weight, up_weight, down_weight))
        slot_grad = lax.optimization_barrier(slot_grad)
        prob_grad = lax.optimization_barrier(prob_grad)
        gate_part = lax.optimization_barrier(gate_part)
        up_part = lax.optimization_barrier(up_part)
        grad_back = to_sources(slot_grad, group_size, EXPERTS, CAP)
        prob_back = to_sources(prob_grad, group_size, EXPERTS, CAP)
        expert_sum, prob_route = jax.vmap(unpacker)(grad_back, prob_back, block_positions)
        new_totals = (totals[0] + gate_part.astype(jnp.float32), totals[1] + up_part.astype(jnp.float32))
        return new_totals, (expert_sum, prob_route)

    zero_grads = jnp.zeros((EXPERTS, D, HID), jnp.float32)
    sums, outputs = lax.scan(one_group, (zero_grads, zero_grads),
                             (group_tokens, group_cotangent, group_probs, group_positions))
    expert_sum = outputs[0].reshape(TOKENS, D)
    prob_route = outputs[1].reshape(TOKENS, TOPK)
    expert_ids = jnp.arange(EXPERTS, dtype=jnp.int32)
    matches = routes[:, :, None] == expert_ids[None, None, :]
    prob_full = jnp.sum(jnp.where(matches, prob_route[:, :, None], jnp.zeros((), jnp.float32)), axis=1)
    logit_grad = router_probs * (prob_full - jnp.sum(router_probs * prob_full, axis=1, keepdims=True))
    token_grad = (expert_sum + jnp.dot(logit_grad, router_weight, precision=highest)).astype(jnp.bfloat16)
    router_grad = jnp.dot(logit_grad.T, tokens.astype(jnp.float32), precision=highest)
    return token_grad, sums[0].astype(jnp.bfloat16), sums[1].astype(jnp.bfloat16), router_grad
```

```python
import jax
import jax.numpy as jnp
from jax import lax
from jax.experimental import pallas as pl
from jax.experimental.pallas import tpu as pltpu
from jax.sharding import Mesh, PartitionSpec as P

f32 = jnp.float32
bf16 = jnp.bfloat16
DP = ("y", "core")
EXPERT = ("x", "z")
CHUNK = 256
ROWS = (((0,), (0,)), ((), ()))
LAST = (((1,), (1,)), ((), ()))
PLAIN = (((1,), (0,)), ((), ()))


def dot(left, right, dims=PLAIN):
    return lax.dot_general(left, right, dims, preferred_element_type=f32)


def split3(value):
    high = value.astype(bf16)
    rest = value - high.astype(f32)
    mid = rest.astype(bf16)
    low = (rest - mid.astype(f32)).astype(bf16)
    return high, mid, low


def dispatch_kernel(routes_ref, mask_ref, tokens_ref, cotangent_ref, sent_ref, select_ref):
    experts, both, _ = sent_ref.shape
    capacity = both // 2
    tok_rows, top_count = routes_ref.shape
    lane = lax.broadcasted_iota(jnp.int32, (tok_rows, experts), 1)
    live = jnp.zeros((tok_rows, experts), f32)
    for k in range(top_count):
        live = live + jnp.where(routes_ref[:, k : k + 1] == lane, 1.0, 0.0)
    row = lax.broadcasted_iota(jnp.int32, (tok_rows, tok_rows), 0)
    column = lax.broadcasted_iota(jnp.int32, (tok_rows, tok_rows), 1)
    same = jnp.where(row == column, 1.0, 0.0).astype(bf16)
    earlier = jnp.where(row < column, 1.0, 0.0).astype(bf16)
    live = dot(live.astype(bf16), same, ROWS)
    live = jnp.where(mask_ref[...] == 1, live, 0.0)
    before = dot(live.astype(bf16), earlier)
    place = jnp.where(live > 0.5, before, -1.0).astype(bf16)
    slots = experts * capacity
    owner = lax.broadcasted_iota(jnp.int32, (slots, experts), 0) // capacity
    spread = jnp.where(owner == lax.broadcasted_iota(jnp.int32, (slots, experts), 1), 1.0, 0.0)
    place = dot(spread.astype(bf16), place)
    index = lax.broadcasted_iota(jnp.int32, (slots, tok_rows), 0) % capacity
    select = jnp.where(place == index.astype(f32), 1.0, 0.0).astype(bf16)
    select_ref[...] = select
    for start in range(0, tokens_ref.shape[1], CHUNK):
        columns = slice(start, start + CHUNK)
        for half, ref in enumerate((tokens_ref, cotangent_ref)):
            packed = dot(select, ref[:, columns]).astype(bf16)
            sent_ref[:, half * capacity : (half + 1) * capacity, columns] = packed.reshape(
                experts, capacity, CHUNK
            )


def delta_kernel(
    expert_ref, slots_ref, weights_ref, router_ref, part_ref, delta_ref, share_ref, term_ref,
    flipped_ref, down_ref,
):
    sources, both, features = slots_ref.shape
    capacity = both // 2
    slots = sources * capacity
    shards, shard_rows, hidden = weights_ref.shape
    part = shard_rows // 3
    narrow = hidden // shards
    experts = router_ref.shape[0]
    slot_tokens = slots_ref[:, :capacity, :].reshape(slots, features)
    slot_cotangent = slots_ref[:, capacity:, :].reshape(slots, features)
    flipped_ref[...] = slot_tokens.T
    down_ref[:, :hidden] = weights_ref[:, 2 * part : 2 * part + narrow, :].reshape(hidden, hidden)
    extra = features - hidden
    pieces = [
        weights_ref[:, 2 * part + narrow :, i * extra : (i + 1) * extra]
        for i in range(hidden // extra)
    ]
    down_ref[:, hidden:] = jnp.stack(pieces, axis=1).reshape(hidden, extra)

    stack = jnp.concatenate(split3(router_ref[...]), axis=0)
    logits = dot(slot_tokens, stack, LAST)
    logits = logits[:, :experts] + (
        logits[:, experts : 2 * experts] + logits[:, 2 * experts :]
    )
    weights = jnp.exp(logits)
    probs = weights / jnp.sum(weights, axis=1, keepdims=True)
    mine = lax.broadcasted_iota(jnp.int32, (slots, experts), 1) == expert_ref[0]
    own = jnp.sum(jnp.where(mine, probs, 0.0), axis=1, keepdims=True)
    rounded = own.astype(bf16).astype(f32)

    prob_grad = jnp.zeros((slots, 1), f32)
    for start in range(0, hidden, CHUNK):
        columns = slice(start, start + CHUNK)
        gate = weights_ref[:, :part, columns].reshape(features, CHUNK)
        up = weights_ref[:, part : 2 * part, columns].reshape(features, CHUNK)
        gate_proj = dot(slot_tokens, gate)
        up_proj = dot(slot_tokens, up)
        hidden_grad = dot(slot_cotangent, down_ref[columns, :], LAST)
        sigmoid_gate = 1.0 / (1.0 + jnp.exp(-gate_proj))
        activated = gate_proj * sigmoid_gate
        slope = sigmoid_gate * (1.0 + gate_proj * (1.0 - sigmoid_gate))
        prob_grad = prob_grad + jnp.sum(
            hidden_grad * activated * up_proj, axis=1, keepdims=True
        )
        scaled = rounded * hidden_grad
        gate_delta = (scaled * up_proj * slope).astype(bf16)
        up_delta = (scaled * activated).astype(bf16)
        delta_ref[:, columns] = gate_delta
        delta_ref[:, hidden + start : hidden + start + CHUNK] = up_delta
        for half, delta in enumerate((gate_delta, up_delta)):
            product = dot(flipped_ref[...], delta).astype(bf16)
            part_ref[:, half * part : (half + 1) * part, columns] = product.reshape(
                shards, part, CHUNK
            )
    share = prob_grad.astype(bf16).astype(f32) * own
    share = share * (jnp.where(mine, 1.0, 0.0) - probs)
    share_ref[...] = share
    term = dot(jnp.concatenate(split3(share), axis=1), slot_tokens, ROWS)
    term_ref[...] = term[:experts] + (term[experts : 2 * experts] + term[2 * experts :])


def slot_grad_kernel(delta_ref, weights_ref, share_ref, router_ref, grad_ref):
    shards, shard_rows, hidden = weights_ref.shape
    part = shard_rows // 3
    features = grad_ref.shape[1]
    step = CHUNK // part
    share_high, share_mid, _ = split3(share_ref[...])
    router_high, router_mid, _ = split3(router_ref[...])
    left = jnp.concatenate([share_high, share_high, share_mid], axis=1)
    right = jnp.concatenate([router_high, router_mid, router_high], axis=0)
    for block in range(features // CHUNK):
        gate = weights_ref[block * step : (block + 1) * step, :part, :].reshape(CHUNK, hidden)
        up = weights_ref[block * step : (block + 1) * step, part : 2 * part, :].reshape(
            CHUNK, hidden
        )
        columns = slice(block * CHUNK, (block + 1) * CHUNK)
        total = dot(delta_ref[:, :hidden], gate, LAST) + dot(delta_ref[:, hidden:], up, LAST)
        grad_ref[:, columns] = (total + dot(left, right[:, columns])).astype(bf16)


def combine_kernel(select_ref, back_ref, out_ref):
    for start in range(0, out_ref.shape[1], CHUNK):
        columns = slice(start, start + CHUNK)
        out_ref[:, columns] = dot(select_ref[...], back_ref[:, columns], ROWS).astype(bf16)


def call(kernel, outs, flops, size, scratch=(), smem=0, name=None):
    def run(*operands):
        vmem = pl.BlockSpec(memory_space=pltpu.VMEM)
        specs = [pl.BlockSpec(memory_space=pltpu.SMEM)] * smem + [vmem] * (len(operands) - smem)
        return pl.pallas_call(
            kernel,
            out_shape=[jax.ShapeDtypeStruct(s, d) for s, d in outs],
            in_specs=specs,
            out_specs=[vmem] * len(outs),
            scratch_shapes=list(scratch),
            compiler_params=pltpu.CompilerParams(vmem_limit_bytes=48 * 1024 * 1024),
            cost_estimate=pl.CostEstimate(flops=flops, bytes_accessed=size, transcendentals=0),
            name=name,
        )(*operands)

    return run


def pack_down(down_shard, hidden):
    extra = down_shard.shape[1] - hidden
    tail = down_shard[:, hidden:].reshape(hidden // extra, -1, extra)
    return jnp.concatenate(
        [down_shard[:, :hidden], jnp.concatenate([t for t in tail], axis=1)], axis=0
    )


def per_device(
    tokens, cotangent, router_weight, gate_weight, up_weight, down_weight, routes, drop_mask
):
    tok_rows, features = tokens.shape
    experts = router_weight.shape[0]
    top_count = routes.shape[1]
    _, part, hidden = gate_weight.shape
    shards = features // part
    capacity = tok_rows * top_count * 2 // (3 * experts)
    slots = experts * capacity

    shard = jnp.concatenate(
        [gate_weight[0], up_weight[0], pack_down(down_weight[0], hidden)], axis=0
    )
    weights = lax.all_gather(shard, DP, axis=0, tiled=True)
    weights = weights.reshape(shards, 3 * part, hidden)

    sent, select = call(
        dispatch_kernel,
        [((experts, 2 * capacity, features), bf16), ((slots, tok_rows), bf16)],
        4 * slots * tok_rows * features,
        3 * 2**20,
        name="dispatch",
    )(routes, drop_mask.reshape(1, tok_rows), tokens, cotangent)
    slot_rows = lax.all_to_all(sent, EXPERT, split_axis=0, concat_axis=0, tiled=True)

    me = lax.axis_index(EXPERT).astype(jnp.int32).reshape(1)
    parts, deltas, share, term = call(
        delta_kernel,
        [
            ((shards, 2 * part, hidden), bf16),
            ((slots, 2 * hidden), bf16),
            ((slots, experts), f32),
            ((experts, features), f32),
        ],
        10 * slots * features * hidden,
        10 * 2**20,
        scratch=[pltpu.VMEM((features, slots), bf16), pltpu.VMEM((hidden, features), bf16)],
        smem=1,
        name="deltas",
    )(me, slot_rows, weights, router_weight)
    sums = lax.psum_scatter(
        parts.reshape(shards * 2 * part, hidden), DP, scatter_dimension=0, tiled=True
    )
    (slot_grad,) = call(
        slot_grad_kernel,
        [((slots, features), bf16)],
        4 * slots * features * hidden,
        6 * 2**20,
        name="slot_grad",
    )(deltas, weights, share, router_weight)
    back = lax.all_to_all(slot_grad, EXPERT, split_axis=0, concat_axis=0, tiled=True)
    (token_grad,) = call(
        combine_kernel,
        [((tok_rows, features), bf16)],
        2 * slots * tok_rows * features,
        2 * 2**20,
        name="combine",
    )(select, back)

    term = lax.all_to_all(term, EXPERT, split_axis=0, concat_axis=0, tiled=True)
    term = jnp.sum(term, axis=0, keepdims=True)
    term = jnp.sum(lax.all_gather(term, DP, axis=0, tiled=True), axis=0, keepdims=True)
    router_grad = lax.all_to_all(
        jnp.broadcast_to(term, (experts, features)), EXPERT, split_axis=0, concat_axis=0, tiled=True
    )
    return token_grad, sums[:part][None], sums[part:][None], router_grad


def solution(mesh):
    fine = Mesh(mesh.devices.reshape(8, 2, 4, 8), DP + EXPERT)
    rows = P(DP + EXPERT, None)
    shard = P(EXPERT, DP, None)
    return jax.shard_map(
        per_device,
        mesh=fine,
        in_specs=(rows, rows, P(), shard, shard, shard, rows, P(DP + EXPERT)),
        out_specs=(rows, shard, shard, P()),
        check_vma=False,
    )
```

```python
import jax
import jax.numpy as jnp
from jax import lax
from jax.experimental import pallas as pl
from jax.experimental.pallas import tpu as pltpu
from jax.sharding import Mesh, PartitionSpec as P

f32 = jnp.float32
bf16 = jnp.bfloat16
DP = ("y", "core")
EXPERT = ("x", "z")
CHUNK = 256
ROWS = (((0,), (0,)), ((), ()))
LAST = (((1,), (1,)), ((), ()))
PLAIN = (((1,), (0,)), ((), ()))


def dot(left, right, dims=PLAIN):
    return lax.dot_general(left, right, dims, preferred_element_type=f32)


def split3(value):
    high = value.astype(bf16)
    rest = value - high.astype(f32)
    mid = rest.astype(bf16)
    low = (rest - mid.astype(f32)).astype(bf16)
    return high, mid, low


def dispatch_kernel(routes_ref, mask_ref, tokens_ref, cotangent_ref, sent_ref, select_ref):
    experts, both, _ = sent_ref.shape
    capacity = both // 2
    tok_rows, top_count = routes_ref.shape
    slots = experts * capacity

    @pl.when(pl.program_id(0) == 0)
    def _():
        lane = lax.broadcasted_iota(jnp.int32, (tok_rows, experts), 1)
        live = jnp.zeros((tok_rows, experts), f32)
        for k in range(top_count):
            live = live + jnp.where(routes_ref[:, k : k + 1] == lane, 1.0, 0.0)
        row = lax.broadcasted_iota(jnp.int32, (tok_rows, tok_rows), 0)
        column = lax.broadcasted_iota(jnp.int32, (tok_rows, tok_rows), 1)
        same = jnp.where(row == column, 1.0, 0.0).astype(bf16)
        earlier = jnp.where(row < column, 1.0, 0.0).astype(bf16)
        live = dot(live.astype(bf16), same, ROWS)
        live = jnp.where(mask_ref[...] == 1, live, 0.0)
        before = dot(live.astype(bf16), earlier)
        place = jnp.where(live > 0.5, before, -1.0).astype(bf16)
        owner = lax.broadcasted_iota(jnp.int32, (slots, experts), 0) // capacity
        spread = jnp.where(owner == lax.broadcasted_iota(jnp.int32, (slots, experts), 1), 1.0, 0.0)
        place = dot(spread.astype(bf16), place)
        index = lax.broadcasted_iota(jnp.int32, (slots, tok_rows), 0) % capacity
        select_ref[...] = jnp.where(place == index.astype(f32), 1.0, 0.0).astype(bf16)

    for half, ref in enumerate((tokens_ref, cotangent_ref)):
        packed = dot(select_ref[...], ref[...]).astype(bf16)
        sent_ref[:, half * capacity : (half + 1) * capacity, :] = packed.reshape(
            experts, capacity, ref.shape[1]
        )


def load_shards(place_ref, shard_refs, weights_ref, sems, rows):
    return [
        pltpu.make_async_copy(
            ref.at[pl.ds(0, rows)], weights_ref.at[place_ref[i]], sems.at[i]
        )
        for i, ref in enumerate(shard_refs)
    ]


def delta_kernel(shards, place_ref, slots_ref, *refs):
    shard_refs = refs[:shards]
    (router_ref, keep_ref, give_ref, delta_ref, share_ref, term_ref,
     weights_ref, flipped_ref, down_ref, sems) = refs[shards:]
    sources, both, features = slots_ref.shape
    capacity = both // 2
    slots = sources * capacity
    _, shard_rows, hidden = weights_ref.shape
    part = shard_rows // 3
    narrow = hidden // shards
    experts = router_ref.shape[0]
    copies = load_shards(place_ref, shard_refs, weights_ref, sems, shard_rows)
    for copy in copies:
        copy.start()
    expert, my_y, my_core = place_ref[shards], place_ref[shards + 1], place_ref[shards + 2]
    slot_tokens = slots_ref[:, :capacity, :].reshape(slots, features)
    slot_cotangent = slots_ref[:, capacity:, :].reshape(slots, features)
    flipped = slot_tokens.T
    ring = shards // 2
    for s in range(shards):
        away = lax.rem(s // 2 - my_y + ring, ring)
        other = jnp.bitwise_xor(my_core, s % 2)
        flipped_ref[other, away] = flipped[s * part : (s + 1) * part, :]

    stack = jnp.concatenate(split3(router_ref[...]), axis=0)
    logits = dot(slot_tokens, stack, LAST)
    logits = logits[:, :experts] + (
        logits[:, experts : 2 * experts] + logits[:, 2 * experts :]
    )
    weights = jnp.exp(logits)
    probs = weights / jnp.sum(weights, axis=1, keepdims=True)
    mine = lax.broadcasted_iota(jnp.int32, (slots, experts), 1) == expert
    own = jnp.sum(jnp.where(mine, probs, 0.0), axis=1, keepdims=True)
    rounded = own.astype(bf16).astype(f32)

    for copy in copies:
        copy.wait()
    down_ref[:, :hidden] = weights_ref[:, 2 * part : 2 * part + narrow, :].reshape(hidden, hidden)
    extra = features - hidden
    pieces = [
        weights_ref[:, 2 * part + narrow :, i * extra : (i + 1) * extra]
        for i in range(hidden // extra)
    ]
    down_ref[:, hidden:] = jnp.stack(pieces, axis=1).reshape(hidden, extra)

    prob_grad = jnp.zeros((slots, 1), f32)
    for start in range(0, hidden, CHUNK):
        columns = slice(start, start + CHUNK)
        gate = weights_ref[:, :part, columns].reshape(features, CHUNK)
        up = weights_ref[:, part : 2 * part, columns].reshape(features, CHUNK)
        gate_proj = dot(slot_tokens, gate)
        up_proj = dot(slot_tokens, up)
        hidden_grad = dot(slot_cotangent, down_ref[columns, :], LAST)
        sigmoid_gate = 1.0 / (1.0 + jnp.exp(-gate_proj))
        activated = gate_proj * sigmoid_gate
        slope = sigmoid_gate * (1.0 + gate_proj * (1.0 - sigmoid_gate))
        prob_grad = prob_grad + jnp.sum(
            hidden_grad * activated * up_proj, axis=1, keepdims=True
        )
        scaled = rounded * hidden_grad
        gate_delta = (scaled * up_proj * slope).astype(bf16)
        up_delta = (scaled * activated).astype(bf16)
        delta_ref[:, columns] = gate_delta
        delta_ref[:, hidden + start : hidden + start + CHUNK] = up_delta
        for half, delta in enumerate((gate_delta, up_delta)):
            for other, ref in enumerate((keep_ref, give_ref)):
                product = dot(flipped_ref[other].reshape(ring * part, slots), delta).astype(bf16)
                ref[:, half * part : (half + 1) * part, columns] = product.reshape(
                    ring, part, CHUNK
                )
    share = prob_grad.astype(bf16).astype(f32) * own
    share = share * (jnp.where(mine, 1.0, 0.0) - probs)
    share_ref[...] = share
    term = dot(jnp.concatenate(split3(share), axis=1), slot_tokens, ROWS)
    term_ref[...] = term[:experts] + (term[experts : 2 * experts] + term[2 * experts :])


def slot_grad_kernel(shards, place_ref, delta_ref, *refs):
    shard_refs = refs[:shards]
    share_ref, router_ref, grad_ref, weights_ref, sems = refs[shards:]
    _, shard_rows, hidden = weights_ref.shape
    part = shard_rows // 2
    features = grad_ref.shape[1]
    step = CHUNK // part
    copies = load_shards(place_ref, shard_refs, weights_ref, sems, shard_rows)
    for copy in copies:
        copy.start()
    share_high, share_mid, _ = split3(share_ref[...])
    router_high, router_mid, _ = split3(router_ref[...])
    left = jnp.concatenate([share_high, share_high, share_mid], axis=1)
    right = jnp.concatenate([router_high, router_mid, router_high], axis=0)
    for copy in copies:
        copy.wait()
    for block in range(features // CHUNK):
        gate = weights_ref[block * step : (block + 1) * step, :part, :].reshape(CHUNK, hidden)
        up = weights_ref[block * step : (block + 1) * step, part:, :].reshape(CHUNK, hidden)
        columns = slice(block * CHUNK, (block + 1) * CHUNK)
        total = dot(delta_ref[:, :hidden], gate, LAST) + dot(delta_ref[:, hidden:], up, LAST)
        grad_ref[:, columns] = (total + dot(left, right[:, columns])).astype(bf16)


def combine_kernel(select_ref, back_ref, out_ref):
    for start in range(0, out_ref.shape[1], CHUNK):
        columns = slice(start, start + CHUNK)
        out_ref[:, columns] = dot(select_ref[...], back_ref[:, columns], ROWS).astype(bf16)


def call(kernel, specs, outs, flops, size, name, scratch=(), **more):
    return pl.pallas_call(
        kernel,
        out_shape=[jax.ShapeDtypeStruct(s, d) for s, d in outs],
        in_specs=specs,
        scratch_shapes=list(scratch),
        compiler_params=pltpu.CompilerParams(vmem_limit_bytes=48 * 1024 * 1024),
        cost_estimate=pl.CostEstimate(flops=flops, bytes_accessed=size, transcendentals=0),
        name=name,
        **more,
    )


SMEM = pl.BlockSpec(memory_space=pltpu.SMEM)
VMEM = pl.BlockSpec(memory_space=pltpu.VMEM)
ANY = pl.BlockSpec(memory_space=pl.ANY)


def pack_down(down_shard, hidden):
    extra = down_shard.shape[1] - hidden
    tail = down_shard[:, hidden:].reshape(hidden // extra, -1, extra)
    return jnp.concatenate(
        [down_shard[:, :hidden], jnp.concatenate([t for t in tail], axis=1)], axis=0
    )


def turn(value, axis, by):
    size = lax.axis_size(axis)
    return lax.ppermute(value, axis, [(i, (i + by) % size) for i in range(size)])


def swap(value, axis, by=1):
    size = lax.axis_size(axis)
    return lax.ppermute(value, axis, [(i, i ^ by) for i in range(size)])


def gather_shards(shard):
    ring = lax.axis_size("y")
    y, core = lax.axis_index("y"), lax.axis_index("core")
    found = {0: shard}
    up = down = shard
    for step in range(1, ring // 2 + 1):
        up = turn(up, "y", 1)
        found[-step] = up
        if step < ring // 2:
            down = turn(down, "y", -1)
            found[step] = down
    arrays, places = [], []
    for away, array in found.items():
        row = lax.rem(y + away + ring, ring) * 2
        arrays += [array, swap(array, "core")]
        places += [row + core, row + 1 - core]
    return arrays, places


def ring_sum(keep, give):
    got = swap(give, "core")
    ring = keep.shape[0]
    half = keep.shape[1] // 2

    def chunk(r):
        return keep[r % ring].astype(f32) + got[r % ring].astype(f32)

    middle = chunk(ring // 2)
    left = turn(middle[:half].astype(bf16), "y", -1)
    right = turn(middle[half:].astype(bf16), "y", 1)
    nothing = jnp.zeros_like(left)
    left = jnp.concatenate([left, nothing], axis=0)
    right = jnp.concatenate([nothing, right], axis=0)
    for r in range(ring // 2 - 1, 0, -1):
        left = turn((chunk(-r) + left.astype(f32)).astype(bf16), "y", -1)
        right = turn((chunk(r) + right.astype(f32)).astype(bf16), "y", 1)
    return (chunk(0) + left.astype(f32) + right.astype(f32)).astype(bf16)


def per_device(
    tokens, cotangent, router_weight, gate_weight, up_weight, down_weight, routes, drop_mask
):
    tok_rows, features = tokens.shape
    experts = router_weight.shape[0]
    top_count = routes.shape[1]
    _, part, hidden = gate_weight.shape
    shards = features // part
    ring = shards // 2
    capacity = tok_rows * top_count * 2 // (3 * experts)
    slots = experts * capacity

    def whole(shape):
        return pl.BlockSpec(shape, lambda i: (0,) * len(shape))

    sent, select = call(
        dispatch_kernel,
        [
            whole((tok_rows, top_count)),
            whole((1, tok_rows)),
            pl.BlockSpec((tok_rows, CHUNK), lambda i: (0, i)),
            pl.BlockSpec((tok_rows, CHUNK), lambda i: (0, i)),
        ],
        [((experts, 2 * capacity, features), bf16), ((slots, tok_rows), bf16)],
        4 * slots * tok_rows * features,
        3 * 2**20,
        "dispatch",
        grid=(features // CHUNK,),
        out_specs=[
            pl.BlockSpec((experts, 2 * capacity, CHUNK), lambda i: (0, 0, i)),
            whole((slots, tok_rows)),
        ],
    )(routes, drop_mask.reshape(1, tok_rows), tokens, cotangent)
    slot_rows = lax.all_to_all(sent, EXPERT, split_axis=0, concat_axis=0, tiled=True)

    shard = jnp.concatenate(
        [gate_weight[0], up_weight[0], pack_down(down_weight[0], hidden)], axis=0
    )
    arrays, places = gather_shards(shard)
    places += [lax.axis_index(EXPERT), lax.axis_index("y"), lax.axis_index("core")]
    place = jnp.stack(places).astype(jnp.int32)

    keep, give, deltas, share, term = call(
        lambda *refs: delta_kernel(shards, *refs),
        [SMEM, VMEM] + [ANY] * shards + [VMEM],
        [
            ((ring, 2 * part, hidden), bf16),
            ((ring, 2 * part, hidden), bf16),
            ((slots, 2 * hidden), bf16),
            ((slots, experts), f32),
            ((experts, features), f32),
        ],
        10 * slots * features * hidden,
        10 * 2**20,
        "deltas",
        scratch=[
            pltpu.VMEM((shards, 3 * part, hidden), bf16),
            pltpu.VMEM((2, ring, part, slots), bf16),
            pltpu.VMEM((hidden, features), bf16),
            pltpu.SemaphoreType.DMA((shards,)),
        ],
    )(place, slot_rows, *arrays, router_weight)
    sums = ring_sum(keep, give)
    (slot_grad,) = call(
        lambda *refs: slot_grad_kernel(shards, *refs),
        [SMEM, VMEM] + [ANY] * shards + [VMEM, VMEM],
        [((slots, features), bf16)],
        4 * slots * features * hidden,
        6 * 2**20,
        "slot_grad",
        scratch=[
            pltpu.VMEM((shards, 2 * part, hidden), bf16),
            pltpu.SemaphoreType.DMA((shards,)),
        ],
    )(place, deltas, *arrays, share, router_weight)

    term = lax.all_to_all(term, EXPERT, split_axis=0, concat_axis=0, tiled=True)
    slot_grad, term = lax.optimization_barrier((slot_grad, term))
    back = lax.all_to_all(slot_grad, EXPERT, split_axis=0, concat_axis=0, tiled=True)
    (token_grad,) = call(
        combine_kernel,
        [VMEM, VMEM],
        [((tok_rows, features), bf16)],
        2 * slots * tok_rows * features,
        2 * 2**20,
        "combine",
    )(select, back)

    term = jnp.sum(term.reshape(experts, -1, 128), axis=0)
    for axis, by in (("core", 1), ("y", 1), ("y", 2), ("y", 4)):
        term = term + swap(term, axis, by)
    term = jnp.broadcast_to(term.reshape(1, features), (experts, features))
    router_grad = lax.all_to_all(term, EXPERT, split_axis=0, concat_axis=0, tiled=True)
    return token_grad, sums[:part][None], sums[part:][None], router_grad


def solution(mesh):
    fine = Mesh(mesh.devices.reshape(8, 2, 4, 8), DP + EXPERT)
    rows = P(DP + EXPERT, None)
    shard = P(EXPERT, DP, None)
    return jax.shard_map(
        per_device,
        mesh=fine,
        in_specs=(rows, rows, P(), shard, shard, shard, rows, P(DP + EXPERT)),
        out_specs=(rows, shard, shard, P()),
        check_vma=False,
    )
```

```python
import jax
import jax.numpy as jnp
from jax import lax
from jax.experimental import pallas as pl
from jax.experimental.pallas import tpu as pltpu
from jax.sharding import Mesh, PartitionSpec as P

f32 = jnp.float32
bf16 = jnp.bfloat16
DP = ("y", "core")
EXPERT = ("x", "z")
CHUNK = 256
ROWS = (((0,), (0,)), ((), ()))
LAST = (((1,), (1,)), ((), ()))
PLAIN = (((1,), (0,)), ((), ()))


def dot(left, right, dims=PLAIN):
    return lax.dot_general(left, right, dims, preferred_element_type=f32)


def split3(value):
    high = value.astype(bf16)
    rest = value - high.astype(f32)
    mid = rest.astype(bf16)
    low = (rest - mid.astype(f32)).astype(bf16)
    return high, mid, low


def dispatch_kernel(
    routes_ref, mask_ref, tokens_ref, cotangent_ref, sent_ref, select_ref,
    tokens, cotangent, packed, select, sems,
):
    experts, both, _ = sent_ref.shape
    capacity = both // 2
    top_count, tok_rows = routes_ref.shape
    slots = experts * capacity
    load_tokens = pltpu.make_async_copy(tokens_ref, tokens, sems.at[0])
    load_cotangent = pltpu.make_async_copy(cotangent_ref, cotangent, sems.at[1])
    load_tokens.start()
    load_cotangent.start()
    owner = lax.broadcasted_iota(jnp.int32, (experts, tok_rows), 0)
    live = jnp.zeros((experts, tok_rows), f32)
    for k in range(top_count):
        live = live + jnp.where(routes_ref[k : k + 1, :] == owner, 1.0, 0.0)
    live = jnp.where(mask_ref[...] == 1, live, 0.0)
    row = lax.broadcasted_iota(jnp.int32, (tok_rows, tok_rows), 0)
    column = lax.broadcasted_iota(jnp.int32, (tok_rows, tok_rows), 1)
    earlier = jnp.where(row < column, 1.0, 0.0).astype(bf16)
    before = dot(live.astype(bf16), earlier)
    place = jnp.where(live > 0.5, before, -1.0).astype(bf16)
    owner = lax.broadcasted_iota(jnp.int32, (slots, experts), 0) // capacity
    spread = jnp.where(owner == lax.broadcasted_iota(jnp.int32, (slots, experts), 1), 1.0, 0.0)
    place = dot(spread.astype(bf16), place)
    index = lax.broadcasted_iota(jnp.int32, (slots, tok_rows), 0) % capacity
    select[...] = jnp.where(place == index.astype(f32), 1.0, 0.0).astype(bf16)
    stores = [pltpu.make_async_copy(select, select_ref, sems.at[2])]
    stores[0].start()
    load_tokens.wait()
    load_cotangent.wait()
    pieces = 4
    step = experts // pieces
    for piece in range(pieces):
        some = slice(piece * step, (piece + 1) * step)
        rows = select[piece * step * capacity : (piece + 1) * step * capacity, :]
        for half, ref in enumerate((tokens, cotangent)):
            packed[some, half * capacity : (half + 1) * capacity, :] = (
                dot(rows, ref[...]).astype(bf16).reshape(step, capacity, ref.shape[1])
            )
        store = pltpu.make_async_copy(packed.at[some], sent_ref.at[some], sems.at[3 + piece])
        store.start()
        stores.append(store)
    for store in stores:
        store.wait()


def order_kernel(shards, place_ref, *refs):
    shard_refs = refs[:shards]
    pair_ref, down_ref = refs[shards:]
    _, both, hidden = pair_ref.shape
    narrow, features = down_ref.shape[1:]
    extra = features - hidden
    for i, ref in enumerate(shard_refs):
        place = place_ref[i]
        pair_ref[place] = ref[:both, :]
        down_ref[place, :, :hidden] = ref[both : both + narrow, :]
        down_ref[place, :, hidden:] = jnp.concatenate(
            [ref[both + narrow :, j * extra : (j + 1) * extra] for j in range(hidden // extra)],
            axis=0,
        )


def delta_kernel(
    place_ref, slots_ref, pair_ref, down_ref, router_ref,
    keep_ref, give_ref, delta_ref, share_ref, term_ref, flipped_ref,
):
    sources, both, features = slots_ref.shape
    capacity = both // 2
    slots = sources * capacity
    shards, part, hidden = pair_ref.shape
    part = part // 2
    experts = router_ref.shape[0]
    expert, my_y, my_core = place_ref[0], place_ref[1], place_ref[2]
    slot_tokens = slots_ref[:, :capacity, :].reshape(slots, features)
    slot_cotangent = slots_ref[:, capacity:, :].reshape(slots, features)
    down = down_ref[...].reshape(hidden, features)
    flipped = slot_tokens.T
    ring = shards // 2
    for s in range(shards):
        away = lax.rem(s // 2 - my_y + ring, ring)
        other = jnp.bitwise_xor(my_core, s % 2)
        flipped_ref[other, away] = flipped[s * part : (s + 1) * part, :]

    stack = jnp.concatenate(split3(router_ref[...]), axis=0)
    logits = dot(slot_tokens, stack, LAST)
    logits = logits[:, :experts] + (
        logits[:, experts : 2 * experts] + logits[:, 2 * experts :]
    )
    weights = jnp.exp(logits)
    probs = weights / jnp.sum(weights, axis=1, keepdims=True)
    mine = lax.broadcasted_iota(jnp.int32, (slots, experts), 1) == expert
    own = jnp.sum(jnp.where(mine, probs, 0.0), axis=1, keepdims=True)
    rounded = own.astype(bf16).astype(f32)

    prob_grad = jnp.zeros((slots, 1), f32)
    for start in range(0, hidden, CHUNK):
        columns = slice(start, start + CHUNK)
        gate = pair_ref[:, :part, columns].reshape(features, CHUNK)
        up = pair_ref[:, part:, columns].reshape(features, CHUNK)
        gate_proj = dot(slot_tokens, gate)
        up_proj = dot(slot_tokens, up)
        hidden_grad = dot(slot_cotangent, down[columns, :], LAST)
        sigmoid_gate = 1.0 / (1.0 + jnp.exp(-gate_proj))
        activated = gate_proj * sigmoid_gate
        slope = sigmoid_gate * (1.0 + gate_proj * (1.0 - sigmoid_gate))
        prob_grad = prob_grad + jnp.sum(
            hidden_grad * activated * up_proj, axis=1, keepdims=True
        )
        scaled = rounded * hidden_grad
        gate_delta = (scaled * up_proj * slope).astype(bf16)
        up_delta = (scaled * activated).astype(bf16)
        delta_ref[:, columns] = gate_delta
        delta_ref[:, hidden + start : hidden + start + CHUNK] = up_delta
        for half, delta in enumerate((gate_delta, up_delta)):
            for other, ref in enumerate((keep_ref, give_ref)):
                product = dot(flipped_ref[other].reshape(ring * part, slots), delta).astype(bf16)
                ref[:, half * part : (half + 1) * part, columns] = product.reshape(
                    ring, part, CHUNK
                )
    share = prob_grad.astype(bf16).astype(f32) * own
    share = share * (jnp.where(mine, 1.0, 0.0) - probs)
    share_ref[...] = share
    term = dot(jnp.concatenate(split3(share), axis=1), slot_tokens, ROWS)
    term = term[:experts] + (term[experts : 2 * experts] + term[2 * experts :])
    for i in range(term_ref.shape[1]):
        term_ref[:, i, :] = term[:, i * 128 : (i + 1) * 128]


def slot_grad_kernel(delta_ref, pair_ref, share_ref, router_ref, grad_ref):
    shards, part, hidden = pair_ref.shape
    part = part // 2
    features = grad_ref.shape[1]
    step = CHUNK // part
    share_high, share_mid, _ = split3(share_ref[...])
    router_high, router_mid, _ = split3(router_ref[...])
    left = jnp.concatenate([share_high, share_high, share_mid], axis=1)
    right = jnp.concatenate([router_high, router_mid, router_high], axis=0)
    for block in range(features // CHUNK):
        gate = pair_ref[block * step : (block + 1) * step, :part, :].reshape(CHUNK, hidden)
        up = pair_ref[block * step : (block + 1) * step, part:, :].reshape(CHUNK, hidden)
        columns = slice(block * CHUNK, (block + 1) * CHUNK)
        total = dot(delta_ref[:, :hidden], gate, LAST) + dot(delta_ref[:, hidden:], up, LAST)
        grad_ref[:, columns] = (total + dot(left, right[:, columns])).astype(bf16)


def message_kernel(keep_ref, got_ref, row_ref, own_ref, *message_refs):
    rows = keep_ref.shape[1]
    own_ref[...] = keep_ref[0].astype(f32) + got_ref[0].astype(f32)
    high, mid, _ = split3(row_ref[...])
    blank = jnp.zeros((row_ref.shape[0], keep_ref.shape[2] - 256), bf16)
    tail = jnp.concatenate([high, mid, blank], axis=1)
    for r, ref in enumerate(message_refs):
        ref[:rows, :] = (keep_ref[r + 1].astype(f32) + got_ref[r + 1].astype(f32)).astype(bf16)
        ref[rows:, :] = tail


def total_kernel(own_ref, row_ref, *refs):
    message_refs = refs[:-3]
    gate_ref, up_ref, total_ref = refs[-3:]
    half = gate_ref.shape[0]
    rows = 2 * half
    row = row_ref[...]
    for ref in message_refs:
        row = row + (ref[rows:, :128].astype(f32) + ref[rows:, 128:256].astype(f32))
    total_ref[...] = row
    for i, out_ref in enumerate((gate_ref, up_ref)):
        some = slice(i * half, (i + 1) * half)
        total = own_ref[some, :]
        for ref in message_refs:
            total = total + ref[some, :].astype(f32)
        out_ref[...] = total.astype(bf16)


def combine_kernel(select_ref, back_ref, out_ref):
    for start in range(0, out_ref.shape[1], CHUNK):
        columns = slice(start, start + CHUNK)
        out_ref[:, columns] = dot(select_ref[...], back_ref[:, columns], ROWS).astype(bf16)


def call(kernel, specs, outs, flops, size, name, mib, scratch=(), **more):
    return pl.pallas_call(
        kernel,
        out_shape=[jax.ShapeDtypeStruct(s, d) for s, d in outs],
        in_specs=specs,
        scratch_shapes=list(scratch),
        compiler_params=pltpu.CompilerParams(vmem_limit_bytes=mib * 2**20),
        cost_estimate=pl.CostEstimate(flops=flops, bytes_accessed=size, transcendentals=0),
        name=name,
        **more,
    )


SMEM = pl.BlockSpec(memory_space=pltpu.SMEM)
VMEM = pl.BlockSpec(memory_space=pltpu.VMEM)
HBM = pl.BlockSpec(memory_space=pltpu.HBM)


def pack_down(down_shard, hidden):
    extra = down_shard.shape[1] - hidden
    tail = down_shard[:, hidden:].reshape(hidden // extra, -1, extra)
    return jnp.concatenate(
        [down_shard[:, :hidden], jnp.concatenate([t for t in tail], axis=1)], axis=0
    )


def turn(value, axis, by):
    size = lax.axis_size(axis)
    return lax.ppermute(value, axis, [(i, (i + by) % size) for i in range(size)])


def swap(value, axis, by=1):
    size = lax.axis_size(axis)
    return lax.ppermute(value, axis, [(i, i ^ by) for i in range(size)])


def gather_shards(shard):
    ring = lax.axis_size("y")
    y, core = lax.axis_index("y"), lax.axis_index("core")
    found = {0: shard}
    up = down = shard
    for step in range(1, ring // 2 + 1):
        up = turn(up, "y", 1)
        found[-step] = up
        if step < ring // 2:
            down = turn(down, "y", -1)
            found[step] = down
    arrays, places = [], []
    for away, array in found.items():
        row = lax.rem(y + away + ring, ring) * 2
        arrays += [array, swap(array, "core")]
        places += [row + core, row + 1 - core]
    return arrays, places


def sum_over_dp(keep, give, row):
    got = swap(give, "core")
    row = row + swap(row, "core")
    ring, rows, hidden = keep.shape
    message = ((rows + row.shape[0], hidden), bf16)
    own, *messages = call(
        message_kernel,
        [VMEM] * 3,
        [((rows, hidden), f32)] + [message] * (ring - 1),
        2**20,
        5 * 2**20,
        "messages",
        16,
    )(keep, got, row)
    found = [None] * (ring - 1)
    for r in (4, 3, 5, 2, 6, 1, 7):
        found[r - 1] = turn(messages[r - 1], "y", r)
    half = ((rows // 2, hidden), bf16)
    return call(
        total_kernel,
        [VMEM] * (ring + 1),
        [half, half, (row.shape, f32)],
        2**20,
        2 * 2**20,
        "totals",
        16,
    )(own, row, *found)


def per_device(
    tokens, cotangent, router_weight, gate_weight, up_weight, down_weight, routes, drop_mask
):
    tok_rows, features = tokens.shape
    experts = router_weight.shape[0]
    top_count = routes.shape[1]
    _, part, hidden = gate_weight.shape
    shards = features // part
    ring = shards // 2
    capacity = tok_rows * top_count * 2 // (3 * experts)
    slots = experts * capacity

    sent, select = call(
        dispatch_kernel,
        [VMEM, VMEM, HBM, HBM],
        [((experts, 2 * capacity, features), bf16), ((slots, tok_rows), bf16)],
        4 * slots * tok_rows * features,
        3 * 2**20,
        "dispatch",
        16,
        scratch=[
            pltpu.VMEM((tok_rows, features), bf16),
            pltpu.VMEM((tok_rows, features), bf16),
            pltpu.VMEM((experts, 2 * capacity, features), bf16),
            pltpu.VMEM((slots, tok_rows), bf16),
            pltpu.SemaphoreType.DMA((7,)),
        ],
        out_specs=[HBM, HBM],
    )(routes.T, drop_mask.reshape(1, tok_rows), tokens, cotangent)
    slot_rows = lax.all_to_all(sent, EXPERT, split_axis=0, concat_axis=0, tiled=True)

    shard = jnp.concatenate(
        [gate_weight[0], up_weight[0], pack_down(down_weight[0], hidden)], axis=0
    )
    arrays, places = gather_shards(shard)
    pair, down = call(
        lambda *refs: order_kernel(shards, *refs),
        [SMEM] + [VMEM] * shards,
        [((shards, 2 * part, hidden), bf16), ((shards, hidden // shards, features), bf16)],
        2**20,
        9 * 2**20,
        "order",
        16,
    )(jnp.stack(places).astype(jnp.int32), *arrays)
    here = jnp.stack([lax.axis_index(EXPERT), lax.axis_index("y"), lax.axis_index("core")])

    keep, give, deltas, share, term = call(
        delta_kernel,
        [SMEM] + [VMEM] * 4,
        [
            ((ring, 2 * part, hidden), bf16),
            ((ring, 2 * part, hidden), bf16),
            ((slots, 2 * hidden), bf16),
            ((slots, experts), f32),
            ((experts, features // 128, 128), f32),
        ],
        10 * slots * features * hidden,
        10 * 2**20,
        "deltas",
        40,
        scratch=[pltpu.VMEM((2, ring, part, slots), bf16)],
    )(here.astype(jnp.int32), slot_rows, pair, down, router_weight)
    (slot_grad,) = call(
        slot_grad_kernel,
        [VMEM] * 4,
        [((slots, features), bf16)],
        4 * slots * features * hidden,
        6 * 2**20,
        "slot_grad",
        24,
    )(deltas, pair, share, router_weight)

    term = lax.all_to_all(term, EXPERT, split_axis=0, concat_axis=0, tiled=True)
    slot_grad, term = lax.optimization_barrier((slot_grad, term))
    back = lax.all_to_all(slot_grad, EXPERT, split_axis=0, concat_axis=0, tiled=True)
    (token_grad,) = call(
        combine_kernel,
        [VMEM, VMEM],
        [((tok_rows, features), bf16)],
        2 * slots * tok_rows * features,
        2 * 2**20,
        "combine",
        16,
    )(select, back)

    gate_grad, up_grad, row = sum_over_dp(keep, give, jnp.sum(term, axis=0))
    row, _ = lax.optimization_barrier((row, back))
    router_grad = lax.all_to_all(
        jnp.broadcast_to(row[None], (experts,) + row.shape),
        EXPERT,
        split_axis=0,
        concat_axis=0,
        tiled=True,
    )
    return token_grad, gate_grad[None], up_grad[None], router_grad.reshape(experts, features)


def solution(mesh):
    fine = Mesh(mesh.devices.reshape(8, 2, 4, 8), DP + EXPERT)
    rows = P(DP + EXPERT, None)
    shard = P(EXPERT, DP, None)
    return jax.shard_map(
        per_device,
        mesh=fine,
        in_specs=(rows, rows, P(), shard, shard, shard, rows, P(DP + EXPERT)),
        out_specs=(rows, shard, shard, P()),
        check_vma=False,
    )
```

```python
import jax
import jax.numpy as jnp
from jax import lax
from jax.experimental import pallas as pl
from jax.experimental.pallas import tpu as pltpu
from jax.sharding import Mesh, PartitionSpec as P

f32 = jnp.float32
bf16 = jnp.bfloat16
DP = ("y", "core")
EXPERT = ("x", "z")
CHUNK = 256
WHOLE_MIB = 63
ZEROTH = 128
FIRST = 896
ROWS = (((0,), (0,)), ((), ()))
LAST = (((1,), (1,)), ((), ()))
PLAIN = (((1,), (0,)), ((), ()))


def dot(left, right, dims=PLAIN):
    return lax.dot_general(left, right, dims, preferred_element_type=f32)


def split3(value):
    high = value.astype(bf16)
    rest = value - high.astype(f32)
    mid = rest.astype(bf16)
    low = (rest - mid.astype(f32)).astype(bf16)
    return high, mid, low


def pack_shard(gate_hbm, up_hbm, down_hbm, shard, sems):
    part, hidden = gate_hbm.shape
    narrow, features = down_hbm.shape
    extra = features - hidden
    lines = part - narrow
    moves = [
        (gate_hbm, shard.at[pl.ds(0, part)]),
        (up_hbm, shard.at[pl.ds(part, part)]),
        (down_hbm.at[:, pl.ds(0, hidden)], shard.at[pl.ds(2 * part, narrow)]),
    ]
    for i in range(hidden // extra):
        moves.append(
            (
                down_hbm.at[pl.ds(i * lines, lines), pl.ds(hidden, extra)],
                shard.at[pl.ds(2 * part + narrow, lines), pl.ds(i * extra, extra)],
            )
        )
    return [
        pltpu.make_async_copy(source, target, sems.at[i])
        for i, (source, target) in enumerate(moves)
    ]


def dispatch_kernel(
    routes_ref, mask_ref, tokens_ref, cotangent_ref, gate_hbm, up_hbm, down_hbm,
    sent_ref, select_ref, shard_hbm, tokens, cotangent, packed, select, shard, sems, shard_sems,
):
    experts, both, _ = sent_ref.shape
    capacity = both // 2
    top_count, tok_rows = routes_ref.shape
    slots = experts * capacity
    load_tokens = pltpu.make_async_copy(tokens_ref, tokens, sems.at[0])
    load_cotangent = pltpu.make_async_copy(cotangent_ref, cotangent, sems.at[1])
    load_tokens.start()
    load_cotangent.start()
    loads = pack_shard(gate_hbm, up_hbm, down_hbm, shard, shard_sems)
    for load in loads:
        load.start()
    owner = lax.broadcasted_iota(jnp.int32, (experts, tok_rows), 0)
    live = jnp.zeros((experts, tok_rows), f32)
    for k in range(top_count):
        live = live + jnp.where(routes_ref[k : k + 1, :] == owner, 1.0, 0.0)
    live = jnp.where(mask_ref[...] == 1, live, 0.0)
    row = lax.broadcasted_iota(jnp.int32, (tok_rows, tok_rows), 0)
    column = lax.broadcasted_iota(jnp.int32, (tok_rows, tok_rows), 1)
    earlier = jnp.where(row < column, 1.0, 0.0).astype(bf16)
    before = dot(live.astype(bf16), earlier)
    place = jnp.where(live > 0.5, before, -1.0).astype(bf16)
    owner = lax.broadcasted_iota(jnp.int32, (slots, experts), 0) // capacity
    spread = jnp.where(owner == lax.broadcasted_iota(jnp.int32, (slots, experts), 1), 1.0, 0.0)
    place = dot(spread.astype(bf16), place)
    index = lax.broadcasted_iota(jnp.int32, (slots, tok_rows), 0) % capacity
    select[...] = jnp.where(place == index.astype(f32), 1.0, 0.0).astype(bf16)
    stores = [pltpu.make_async_copy(select, select_ref, sems.at[2])]
    stores[0].start()
    load_tokens.wait()
    load_cotangent.wait()
    pieces = 4
    step = experts // pieces
    for piece in range(pieces):
        some = slice(piece * step, (piece + 1) * step)
        rows = select[piece * step * capacity : (piece + 1) * step * capacity, :]
        for half, ref in enumerate((tokens, cotangent)):
            packed[some, half * capacity : (half + 1) * capacity, :] = (
                dot(rows, ref[...]).astype(bf16).reshape(step, capacity, ref.shape[1])
            )
        store = pltpu.make_async_copy(packed.at[some], sent_ref.at[some], sems.at[3 + piece])
        store.start()
        stores.append(store)
        if piece == 0:
            for load in loads:
                load.wait()
            stores.append(pltpu.make_async_copy(shard, shard_hbm, sems.at[3 + pieces]))
            stores[-1].start()
    for store in stores:
        store.wait()


def expert_kernel(
    expert_ref, slots_ref, router_ref, weights_hbm,
    part_hbm, zeroth_ref, first_ref, second_ref,
    pair_ref, loaded_ref, down_ref, flipped_ref, part_ref, delta_ref, term_ref, sems,
):
    sources, both, features = slots_ref.shape
    capacity = both // 2
    slots = sources * capacity
    chunks, shards, part, _ = pair_ref.shape
    part = part // 2
    hidden = chunks * CHUNK
    narrow = hidden // shards
    extra = features - hidden
    experts = router_ref.shape[0]
    loads = [
        pltpu.make_async_copy(
            weights_hbm.at[:, pl.ds(0, 2 * part), pl.ds(i * CHUNK, CHUNK)],
            pair_ref.at[i],
            sems.at[i],
        )
        for i in range(chunks)
    ]
    load_down = pltpu.make_async_copy(
        weights_hbm.at[:, pl.ds(2 * part, part), :], loaded_ref, sems.at[chunks]
    )
    loads[0].start()
    load_down.start()
    for load in loads[1:]:
        load.start()
    slot_tokens = slots_ref[:, :capacity, :].reshape(slots, features)
    slot_cotangent = slots_ref[:, capacity:, :].reshape(slots, features)
    flipped_ref[...] = slot_tokens.T

    router_high, router_mid, router_low = split3(router_ref[...])
    stack = jnp.concatenate([router_high, router_mid, router_low], axis=0)
    logits = dot(slot_tokens, stack, LAST)
    logits = logits[:, :experts] + (
        logits[:, experts : 2 * experts] + logits[:, 2 * experts :]
    )
    weights = jnp.exp(logits)
    probs = weights / jnp.sum(weights, axis=1, keepdims=True)
    mine = lax.broadcasted_iota(jnp.int32, (slots, experts), 1) == expert_ref[0]
    own = jnp.sum(jnp.where(mine, probs, 0.0), axis=1, keepdims=True)
    rounded = own.astype(bf16).astype(f32)

    prob_grad = jnp.zeros((slots, 1), f32)
    stores = []
    for i, load in enumerate(loads):
        start = i * CHUNK
        columns = slice(start, start + CHUNK)
        load.wait()
        gate = pair_ref[i, :, :part, :].reshape(features, CHUNK)
        up = pair_ref[i, :, part:, :].reshape(features, CHUNK)
        gate_proj = dot(slot_tokens, gate)
        up_proj = dot(slot_tokens, up)
        if i == 0:
            load_down.wait()
            down_ref[:, :hidden] = loaded_ref[:, :narrow, :].reshape(hidden, hidden)
            pieces = [
                loaded_ref[:, narrow:, j * extra : (j + 1) * extra] for j in range(hidden // extra)
            ]
            down_ref[:, hidden:] = jnp.stack(pieces, axis=1).reshape(hidden, extra)
        hidden_grad = dot(slot_cotangent, down_ref[columns, :], LAST)
        sigmoid_gate = 1.0 / (1.0 + jnp.exp(-gate_proj))
        activated = gate_proj * sigmoid_gate
        slope = sigmoid_gate * (1.0 + gate_proj * (1.0 - sigmoid_gate))
        prob_grad = prob_grad + jnp.sum(
            hidden_grad * activated * up_proj, axis=1, keepdims=True
        )
        scaled = rounded * hidden_grad
        gate_delta = (scaled * up_proj * slope).astype(bf16)
        up_delta = (scaled * activated).astype(bf16)
        delta_ref[0, i] = gate_delta
        delta_ref[1, i] = up_delta
        for half, delta in enumerate((gate_delta, up_delta)):
            product = dot(flipped_ref[...], delta).astype(bf16)
            part_ref[:, half * part : (half + 1) * part, columns] = product.reshape(
                shards, part, CHUNK
            )
        stores.append(
            pltpu.make_async_copy(
                part_ref.at[:, :, pl.ds(start, CHUNK)],
                part_hbm.at[:, :, pl.ds(start, CHUNK)],
                sems.at[chunks + 1 + i],
            )
        )
        stores[-1].start()
    share = prob_grad.astype(bf16).astype(f32) * own
    share = share * (jnp.where(mine, 1.0, 0.0) - probs)
    share_high, share_mid, share_low = split3(share)
    term = dot(jnp.concatenate([share_high, share_mid, share_low], axis=1), slot_tokens, ROWS)
    term = term[:experts] + (term[experts : 2 * experts] + term[2 * experts :])
    term_high, term_mid, _ = split3(term)
    for i in range(features // 128):
        columns = slice(i * 128, (i + 1) * 128)
        term_ref[:, i, :] = term_high[:, columns].astype(f32)
        term_ref[:, capacity // 2 + i, :] = term_mid[:, columns].astype(f32)
    zeroth_ref[:, ZEROTH:] = term_ref[...].astype(bf16).reshape(slots, 128)

    left = jnp.concatenate([share_high, share_high, share_mid], axis=1)
    right = jnp.concatenate([router_high, router_mid, router_high], axis=0)
    step = CHUNK // part
    for block in range(features // CHUNK):
        some = slice(block * step, (block + 1) * step)
        start = block * CHUNK
        total = dot(left, right[:, start : start + CHUNK])
        for i in range(chunks):
            gate = pair_ref[i, some, :part, :].reshape(CHUNK, CHUNK)
            up = pair_ref[i, some, part:, :].reshape(CHUNK, CHUNK)
            total = total + dot(delta_ref[0, i], gate, LAST) + dot(delta_ref[1, i], up, LAST)
        total = total.astype(bf16)
        for ref, low, high in (
            (zeroth_ref, 0, ZEROTH),
            (first_ref, ZEROTH, FIRST),
            (second_ref, FIRST, features),
        ):
            begin, end = max(low, start), min(high, start + CHUNK)
            if begin < end:
                ref[:, begin - low : end - low] = total[:, begin - start : end - start]
    for store in stores:
        store.wait()


def fill_kernel(row_ref, given_hbm, second_hbm, block_ref, sem):
    high, mid, _ = split3(row_ref[...])
    block = jnp.concatenate([high.astype(f32), mid.astype(f32)], axis=0).astype(bf16)
    block_ref[...] = jnp.concatenate([block] * (block_ref.shape[0] // block.shape[0]), axis=0)
    place = pl.ds(given_hbm.shape[1] - block.shape[1], block.shape[1])
    store = pltpu.make_async_copy(block_ref, second_hbm.at[:, place], sem)
    store.start()
    store.wait()


def combine_kernel(
    select_ref, zeroth_ref, first_ref, second_ref, sums_ref, out_ref, router_ref, gate_ref, up_ref
):
    experts, features = router_ref.shape
    slots = select_ref.shape[0]
    select = select_ref[...]
    rest = features - FIRST
    out_ref[:, :ZEROTH] = dot(select, zeroth_ref[:, :ZEROTH], ROWS).astype(bf16)
    out_ref[:, ZEROTH:FIRST] = dot(select, first_ref[...], ROWS).astype(bf16)
    out_ref[:, FIRST:] = dot(select, second_ref[:, :rest], ROWS).astype(bf16)
    rows = second_ref[:, rest:].astype(f32).reshape(experts, slots // experts, 128)
    half = slots // experts // 2
    rows = rows[:, :half, :] + rows[:, half:, :]
    for i in range(half):
        router_ref[:, i * 128 : (i + 1) * 128] = rows[:, i, :]
    part = gate_ref.shape[0]
    gate_ref[...] = sums_ref[:part, :]
    up_ref[...] = sums_ref[part:, :]


def call(kernel, specs, outs, flops, size, name, mib, scratch=(), **more):
    return pl.pallas_call(
        kernel,
        out_shape=[jax.ShapeDtypeStruct(s, d) for s, d in outs],
        in_specs=specs,
        scratch_shapes=list(scratch),
        compiler_params=pltpu.CompilerParams(vmem_limit_bytes=int(mib * 2**20)),
        cost_estimate=pl.CostEstimate(flops=flops, bytes_accessed=size, transcendentals=0),
        name=name,
        **more,
    )


SMEM = pl.BlockSpec(memory_space=pltpu.SMEM)
VMEM = pl.BlockSpec(memory_space=pltpu.VMEM)
HBM = pl.BlockSpec(memory_space=pltpu.HBM)


def per_device(
    tokens, cotangent, router_weight, gate_weight, up_weight, down_weight, routes, drop_mask
):
    tok_rows, features = tokens.shape
    experts = router_weight.shape[0]
    top_count = routes.shape[1]
    _, part, hidden = gate_weight.shape
    shards = features // part
    capacity = tok_rows * top_count * 2 // (3 * experts)
    slots = experts * capacity

    sent, select, shard = call(
        dispatch_kernel,
        [VMEM, VMEM] + [HBM] * 5,
        [
            ((experts, 2 * capacity, features), bf16),
            ((slots, tok_rows), bf16),
            ((3 * part, hidden), bf16),
        ],
        4 * slots * tok_rows * features,
        3 * 2**20,
        "dispatch",
        WHOLE_MIB,
        scratch=[
            pltpu.VMEM((tok_rows, features), bf16),
            pltpu.VMEM((tok_rows, features), bf16),
            pltpu.VMEM((experts, 2 * capacity, features), bf16),
            pltpu.VMEM((slots, tok_rows), bf16),
            pltpu.VMEM((3 * part, hidden), bf16),
            pltpu.SemaphoreType.DMA((8,)),
            pltpu.SemaphoreType.DMA((3 + hidden // (features - hidden),)),
        ],
        out_specs=[HBM] * 3,
    )(
        routes.T,
        drop_mask.reshape(1, tok_rows),
        tokens,
        cotangent,
        gate_weight[0],
        up_weight[0],
        down_weight[0],
    )

    slot_rows = lax.all_to_all(sent, EXPERT, split_axis=0, concat_axis=0, tiled=True)
    weights = lax.all_gather(shard, DP, axis=0, tiled=True).reshape(shards, 3 * part, hidden)

    expert = lax.axis_index(EXPERT).astype(jnp.int32).reshape(1)
    chunks = hidden // CHUNK
    second_width = features - FIRST + 128
    parts, zeroth, first, second = call(
        expert_kernel,
        [SMEM, VMEM, VMEM, HBM],
        [
            ((shards, 2 * part, hidden), bf16),
            ((slots, ZEROTH + 128), bf16),
            ((slots, FIRST - ZEROTH), bf16),
            ((slots, second_width), bf16),
        ],
        14 * slots * features * hidden,
        10 * 2**20,
        "expert",
        48,
        scratch=[
            pltpu.VMEM((chunks, shards, 2 * part, CHUNK), bf16),
            pltpu.VMEM((shards, part, hidden), bf16),
            pltpu.VMEM((hidden, features), bf16),
            pltpu.VMEM((features, slots), bf16),
            pltpu.VMEM((shards, 2 * part, hidden), bf16),
            pltpu.VMEM((2, chunks, slots, CHUNK), bf16),
            pltpu.VMEM((experts, capacity, 128), f32),
            pltpu.SemaphoreType.DMA((1 + 2 * chunks,)),
        ],
        out_specs=[HBM, VMEM, VMEM, VMEM],
    )(expert, slot_rows, router_weight, weights)
    sums = lax.psum_scatter(
        parts.reshape(shards * 2 * part, hidden), DP, scatter_dimension=0, tiled=True
    )

    zeroth = lax.all_to_all(zeroth, EXPERT, split_axis=0, concat_axis=0, tiled=True)
    first, zeroth = lax.optimization_barrier((first, zeroth))
    first = lax.all_to_all(first, EXPERT, split_axis=0, concat_axis=0, tiled=True)
    term = zeroth.reshape(experts, capacity, -1)[:, :, ZEROTH:].astype(f32)
    term = jnp.sum(term.reshape(experts, 2, capacity // 2, 128), axis=(0, 1))
    row = jnp.sum(lax.all_gather(term, DP, axis=0), axis=0)
    row, first = lax.optimization_barrier((row, first))
    (second,) = call(
        fill_kernel,
        [VMEM, HBM],
        [((slots, second_width), bf16)],
        2**17,
        2**17,
        "fill",
        16,
        scratch=[pltpu.VMEM((slots, 128), bf16), pltpu.SemaphoreType.DMA],
        out_specs=[HBM],
        input_output_aliases={1: 0},
    )(row, second)
    second = lax.all_to_all(second, EXPERT, split_axis=0, concat_axis=0, tiled=True)
    token_grad, router_grad, gate_grad, up_grad = call(
        combine_kernel,
        [VMEM] * 5,
        [
            ((tok_rows, features), bf16),
            ((experts, features), f32),
            ((part, hidden), bf16),
            ((part, hidden), bf16),
        ],
        2 * slots * tok_rows * features,
        2 * 2**20,
        "combine",
        16,
    )(select, zeroth, first, second, sums)
    return token_grad, gate_grad[None], up_grad[None], router_grad


def solution(mesh):
    fine = Mesh(mesh.devices.reshape(8, 2, 4, 8), DP + EXPERT)
    rows = P(DP + EXPERT, None)
    shard = P(EXPERT, DP, None)
    return jax.shard_map(
        per_device,
        mesh=fine,
        in_specs=(rows, rows, P(), shard, shard, shard, rows, P(DP + EXPERT)),
        out_specs=(rows, shard, shard, P()),
        check_vma=False,
    )
```

```python
import jax
import jax.numpy as jnp
from jax import lax
from jax.experimental import pallas as pl
from jax.experimental.pallas import tpu as pltpu
from jax.sharding import Mesh, PartitionSpec as P

f32 = jnp.float32
bf16 = jnp.bfloat16
DP = ("y", "core")
EXPERT = ("x", "z")
CHUNK = 256
WHOLE_MIB = 63
ZEROTH = 128
FIRST = 896
ROWS = (((0,), (0,)), ((), ()))
LAST = (((1,), (1,)), ((), ()))
PLAIN = (((1,), (0,)), ((), ()))


def dot(left, right, dims=PLAIN):
    return lax.dot_general(left, right, dims, preferred_element_type=f32)


def split3(value):
    high = value.astype(bf16)
    rest = value - high.astype(f32)
    mid = rest.astype(bf16)
    low = (rest - mid.astype(f32)).astype(bf16)
    return high, mid, low


def pack_shard(gate_hbm, up_hbm, down_hbm, shard, sems):
    part, hidden = gate_hbm.shape
    narrow, features = down_hbm.shape
    extra = features - hidden
    lines = part - narrow
    moves = [
        (gate_hbm, shard.at[pl.ds(0, part)]),
        (up_hbm, shard.at[pl.ds(part, part)]),
        (down_hbm.at[:, pl.ds(0, hidden)], shard.at[pl.ds(2 * part, narrow)]),
    ]
    for i in range(hidden // extra):
        moves.append(
            (
                down_hbm.at[pl.ds(i * lines, lines), pl.ds(hidden, extra)],
                shard.at[pl.ds(2 * part + narrow, lines), pl.ds(i * extra, extra)],
            )
        )
    return [
        pltpu.make_async_copy(source, target, sems.at[i])
        for i, (source, target) in enumerate(moves)
    ]


def dispatch_kernel(
    routes_ref, mask_ref, tokens_ref, cotangent_ref, gate_hbm, up_hbm, down_hbm,
    sent_ref, select_ref, shard_hbm, tokens, cotangent, packed, select, shard, sems, shard_sems,
):
    experts, both, _ = sent_ref.shape
    capacity = both // 2
    top_count, tok_rows = routes_ref.shape
    slots = experts * capacity
    load_tokens = pltpu.make_async_copy(tokens_ref, tokens, sems.at[0])
    load_cotangent = pltpu.make_async_copy(cotangent_ref, cotangent, sems.at[1])
    load_tokens.start()
    load_cotangent.start()
    loads = pack_shard(gate_hbm, up_hbm, down_hbm, shard, shard_sems)
    for load in loads:
        load.start()
    owner = lax.broadcasted_iota(jnp.int32, (experts, tok_rows), 0)
    live = jnp.zeros((experts, tok_rows), f32)
    for k in range(top_count):
        live = live + jnp.where(routes_ref[k : k + 1, :] == owner, 1.0, 0.0)
    live = jnp.where(mask_ref[...] == 1, live, 0.0)
    row = lax.broadcasted_iota(jnp.int32, (tok_rows, tok_rows), 0)
    column = lax.broadcasted_iota(jnp.int32, (tok_rows, tok_rows), 1)
    earlier = jnp.where(row < column, 1.0, 0.0).astype(bf16)
    before = dot(live.astype(bf16), earlier)
    place = jnp.where(live > 0.5, before, -1.0).astype(bf16)
    owner = lax.broadcasted_iota(jnp.int32, (slots, experts), 0) // capacity
    spread = jnp.where(owner == lax.broadcasted_iota(jnp.int32, (slots, experts), 1), 1.0, 0.0)
    place = dot(spread.astype(bf16), place)
    index = lax.broadcasted_iota(jnp.int32, (slots, tok_rows), 0) % capacity
    select[...] = jnp.where(place == index.astype(f32), 1.0, 0.0).astype(bf16)
    stores = [pltpu.make_async_copy(select, select_ref, sems.at[2])]
    stores[0].start()
    load_tokens.wait()
    load_cotangent.wait()
    pieces = 4
    step = experts // pieces
    for piece in range(pieces):
        some = slice(piece * step, (piece + 1) * step)
        rows = select[piece * step * capacity : (piece + 1) * step * capacity, :]
        for half, ref in enumerate((tokens, cotangent)):
            packed[some, half * capacity : (half + 1) * capacity, :] = (
                dot(rows, ref[...]).astype(bf16).reshape(step, capacity, ref.shape[1])
            )
        store = pltpu.make_async_copy(packed.at[some], sent_ref.at[some], sems.at[3 + piece])
        store.start()
        stores.append(store)
        if piece == 0:
            for load in loads:
                load.wait()
            stores.append(pltpu.make_async_copy(shard, shard_hbm, sems.at[3 + pieces]))
            stores[-1].start()
    for store in stores:
        store.wait()


def expert_kernel(
    expert_ref, slots_ref, router_ref, weights_hbm,
    part_hbm, zeroth_ref, first_ref, second_ref,
    pair_ref, down_ref, flipped_ref, part_ref, delta_ref, term_ref, sems,
):
    sources, both, features = slots_ref.shape
    capacity = both // 2
    slots = sources * capacity
    chunks, shards, part, _ = pair_ref.shape
    part = part // 2
    hidden = chunks * CHUNK
    narrow = hidden // shards
    extra = features - hidden
    experts = router_ref.shape[0]
    lines = part - narrow
    steps = 1 + hidden // extra
    loads, known = [], 0
    for i in range(chunks):
        until = -(-(i + 1) * CHUNK // narrow)
        some = pl.ds(known, until - known)
        known = until
        moves = [
            (weights_hbm.at[:, pl.ds(0, 2 * part), pl.ds(i * CHUNK, CHUNK)], pair_ref.at[i]),
            (
                weights_hbm.at[some, pl.ds(2 * part, narrow), :],
                down_ref.at[some, :, pl.ds(0, hidden)],
            ),
        ]
        for j in range(hidden // extra):
            moves.append(
                (
                    weights_hbm.at[some, pl.ds(2 * part + narrow, lines), pl.ds(j * extra, extra)],
                    down_ref.at[some, pl.ds(j * lines, lines), pl.ds(hidden, extra)],
                )
            )
        loads.append(
            [
                pltpu.make_async_copy(source, target, sems.at[i * (1 + steps) + k])
                for k, (source, target) in enumerate(moves)
            ]
        )
    for load in loads:
        for piece in load:
            piece.start()
    slot_tokens = slots_ref[:, :capacity, :].reshape(slots, features)
    slot_cotangent = slots_ref[:, capacity:, :].reshape(slots, features)
    flipped_ref[...] = slot_tokens.T

    router_high, router_mid, router_low = split3(router_ref[...])
    stack = jnp.concatenate([router_high, router_mid, router_low], axis=0)
    logits = dot(slot_tokens, stack, LAST)
    logits = logits[:, :experts] + (
        logits[:, experts : 2 * experts] + logits[:, 2 * experts :]
    )
    weights = jnp.exp(logits)
    probs = weights / jnp.sum(weights, axis=1, keepdims=True)
    mine = lax.broadcasted_iota(jnp.int32, (slots, experts), 1) == expert_ref[0]
    own = jnp.sum(jnp.where(mine, probs, 0.0), axis=1, keepdims=True)
    rounded = own.astype(bf16).astype(f32)

    prob_grad = jnp.zeros((slots, 1), f32)
    stores, todo = [], []
    for i, load in enumerate(loads):
        start = i * CHUNK
        columns = slice(start, start + CHUNK)
        if i == 0:
            load[0].wait()
        gate = pair_ref[i, :, :part, :].reshape(features, CHUNK)
        up = pair_ref[i, :, part:, :].reshape(features, CHUNK)
        gate_proj = dot(slot_tokens, gate)
        up_proj = dot(slot_tokens, up)
        if i == 0:
            for piece in load[1:] + loads[1] + loads[2]:
                piece.wait()
        pieces, row = [], start
        while row < start + CHUNK:
            shard, inside = row // narrow, row % narrow
            end = min(narrow, inside + start + CHUNK - row)
            pieces.append(down_ref[shard, inside:end, :])
            row += end - inside
        hidden_grad = dot(slot_cotangent, jnp.concatenate(pieces, axis=0), LAST)
        sigmoid_gate = 1.0 / (1.0 + jnp.exp(-gate_proj))
        activated = gate_proj * sigmoid_gate
        slope = sigmoid_gate * (1.0 + gate_proj * (1.0 - sigmoid_gate))
        prob_grad = prob_grad + jnp.sum(
            hidden_grad * activated * up_proj, axis=1, keepdims=True
        )
        scaled = rounded * hidden_grad
        gate_delta = (scaled * up_proj * slope).astype(bf16)
        up_delta = (scaled * activated).astype(bf16)
        delta_ref[0, i] = gate_delta
        delta_ref[1, i] = up_delta
        todo.append((start, gate_delta, up_delta))
    for i, (start, *pair) in enumerate(todo):
        columns = slice(start, start + CHUNK)
        for half, delta in enumerate(pair):
            product = dot(flipped_ref[...], delta).astype(bf16)
            part_ref[:, half * part : (half + 1) * part, columns] = product.reshape(
                shards, part, CHUNK
            )
        stores.append(
            pltpu.make_async_copy(
                part_ref.at[:, :, pl.ds(start, CHUNK)],
                part_hbm.at[:, :, pl.ds(start, CHUNK)],
                sems.at[i],
            )
        )
        stores[-1].start()
    share = prob_grad.astype(bf16).astype(f32) * own
    share = share * (jnp.where(mine, 1.0, 0.0) - probs)
    share_high, share_mid, share_low = split3(share)
    term = dot(jnp.concatenate([share_high, share_mid, share_low], axis=1), slot_tokens, ROWS)
    term = term[:experts] + (term[experts : 2 * experts] + term[2 * experts :])
    term_high, term_mid, _ = split3(term)
    for i in range(features // 128):
        columns = slice(i * 128, (i + 1) * 128)
        term_ref[:, i, :] = term_high[:, columns].astype(f32)
        term_ref[:, capacity // 2 + i, :] = term_mid[:, columns].astype(f32)
    zeroth_ref[:, ZEROTH:] = term_ref[...].astype(bf16).reshape(slots, 128)

    left = jnp.concatenate([share_high, share_high, share_mid], axis=1)
    right = jnp.concatenate([router_high, router_mid, router_high], axis=0)
    step = CHUNK // part
    for block in range(features // CHUNK):
        some = slice(block * step, (block + 1) * step)
        start = block * CHUNK
        total = dot(left, right[:, start : start + CHUNK])
        for i in range(chunks):
            gate = pair_ref[i, some, :part, :].reshape(CHUNK, CHUNK)
            up = pair_ref[i, some, part:, :].reshape(CHUNK, CHUNK)
            total = total + dot(delta_ref[0, i], gate, LAST) + dot(delta_ref[1, i], up, LAST)
        total = total.astype(bf16)
        for ref, low, high in (
            (zeroth_ref, 0, ZEROTH),
            (first_ref, ZEROTH, FIRST),
            (second_ref, FIRST, features),
        ):
            begin, end = max(low, start), min(high, start + CHUNK)
            if begin < end:
                ref[:, begin - low : end - low] = total[:, begin - start : end - start]
    for store in stores:
        store.wait()


def fill_kernel(row_ref, given_hbm, second_hbm, block_ref, sem):
    high, mid, _ = split3(row_ref[...])
    block = jnp.concatenate([high.astype(f32), mid.astype(f32)], axis=0).astype(bf16)
    block_ref[...] = jnp.concatenate([block] * (block_ref.shape[0] // block.shape[0]), axis=0)
    place = pl.ds(given_hbm.shape[1] - block.shape[1], block.shape[1])
    store = pltpu.make_async_copy(block_ref, second_hbm.at[:, place], sem)
    store.start()
    store.wait()


def combine_kernel(
    select_ref, zeroth_ref, first_ref, second_ref, sums_ref, out_ref, router_ref, gate_ref, up_ref
):
    experts, features = router_ref.shape
    slots = select_ref.shape[0]
    select = select_ref[...]
    rest = features - FIRST
    out_ref[:, :ZEROTH] = dot(select, zeroth_ref[:, :ZEROTH], ROWS).astype(bf16)
    out_ref[:, ZEROTH:FIRST] = dot(select, first_ref[...], ROWS).astype(bf16)
    out_ref[:, FIRST:] = dot(select, second_ref[:, :rest], ROWS).astype(bf16)
    rows = second_ref[:, rest:].astype(f32).reshape(experts, slots // experts, 128)
    half = slots // experts // 2
    rows = rows[:, :half, :] + rows[:, half:, :]
    for i in range(half):
        router_ref[:, i * 128 : (i + 1) * 128] = rows[:, i, :]
    part = gate_ref.shape[0]
    gate_ref[...] = sums_ref[:part, :]
    up_ref[...] = sums_ref[part:, :]


def call(kernel, specs, outs, flops, size, name, mib, scratch=(), **more):
    return pl.pallas_call(
        kernel,
        out_shape=[jax.ShapeDtypeStruct(s, d) for s, d in outs],
        in_specs=specs,
        scratch_shapes=list(scratch),
        compiler_params=pltpu.CompilerParams(vmem_limit_bytes=int(mib * 2**20)),
        cost_estimate=pl.CostEstimate(flops=flops, bytes_accessed=size, transcendentals=0),
        name=name,
        **more,
    )


SMEM = pl.BlockSpec(memory_space=pltpu.SMEM)
VMEM = pl.BlockSpec(memory_space=pltpu.VMEM)
HBM = pl.BlockSpec(memory_space=pltpu.HBM)


def per_device(
    tokens, cotangent, router_weight, gate_weight, up_weight, down_weight, routes, drop_mask
):
    tok_rows, features = tokens.shape
    experts = router_weight.shape[0]
    top_count = routes.shape[1]
    _, part, hidden = gate_weight.shape
    shards = features // part
    capacity = tok_rows * top_count * 2 // (3 * experts)
    slots = experts * capacity

    sent, select, shard = call(
        dispatch_kernel,
        [VMEM, VMEM] + [HBM] * 5,
        [
            ((experts, 2 * capacity, features), bf16),
            ((slots, tok_rows), bf16),
            ((3 * part, hidden), bf16),
        ],
        4 * slots * tok_rows * features,
        3 * 2**20,
        "dispatch",
        WHOLE_MIB,
        scratch=[
            pltpu.VMEM((tok_rows, features), bf16),
            pltpu.VMEM((tok_rows, features), bf16),
            pltpu.VMEM((experts, 2 * capacity, features), bf16),
            pltpu.VMEM((slots, tok_rows), bf16),
            pltpu.VMEM((3 * part, hidden), bf16),
            pltpu.SemaphoreType.DMA((8,)),
            pltpu.SemaphoreType.DMA((3 + hidden // (features - hidden),)),
        ],
        out_specs=[HBM] * 3,
    )(
        routes.T,
        drop_mask.reshape(1, tok_rows),
        tokens,
        cotangent,
        gate_weight[0],
        up_weight[0],
        down_weight[0],
    )

    slot_rows = lax.all_to_all(sent, EXPERT, split_axis=0, concat_axis=0, tiled=True)
    weights = lax.all_gather(shard, DP, axis=0, tiled=True).reshape(shards, 3 * part, hidden)

    expert = lax.axis_index(EXPERT).astype(jnp.int32).reshape(1)
    chunks = hidden // CHUNK
    second_width = features - FIRST + 128
    parts, zeroth, first, second = call(
        expert_kernel,
        [SMEM, VMEM, VMEM, HBM],
        [
            ((shards, 2 * part, hidden), bf16),
            ((slots, ZEROTH + 128), bf16),
            ((slots, FIRST - ZEROTH), bf16),
            ((slots, second_width), bf16),
        ],
        14 * slots * features * hidden,
        10 * 2**20,
        "expert",
        48,
        scratch=[
            pltpu.VMEM((chunks, shards, 2 * part, CHUNK), bf16),
            pltpu.VMEM((shards, hidden // shards, features), bf16),
            pltpu.VMEM((features, slots), bf16),
            pltpu.VMEM((shards, 2 * part, hidden), bf16),
            pltpu.VMEM((2, chunks, slots, CHUNK), bf16),
            pltpu.VMEM((experts, capacity, 128), f32),
            pltpu.SemaphoreType.DMA((chunks * (2 + hidden // (features - hidden)),)),
        ],
        out_specs=[HBM, VMEM, VMEM, VMEM],
    )(expert, slot_rows, router_weight, weights)
    sums = lax.psum_scatter(
        parts.reshape(shards * 2 * part, hidden), DP, scatter_dimension=0, tiled=True
    )

    zeroth = lax.all_to_all(zeroth, EXPERT, split_axis=0, concat_axis=0, tiled=True)
    first, zeroth = lax.optimization_barrier((first, zeroth))
    first = lax.all_to_all(first, EXPERT, split_axis=0, concat_axis=0, tiled=True)
    term = zeroth.reshape(experts, capacity, -1)[:, :, ZEROTH:].astype(f32)
    term = jnp.sum(term.reshape(experts, 2, capacity // 2, 128), axis=(0, 1))
    row = jnp.sum(lax.all_gather(term, DP, axis=0), axis=0)
    row, first = lax.optimization_barrier((row, first))
    (second,) = call(
        fill_kernel,
        [VMEM, HBM],
        [((slots, second_width), bf16)],
        2**17,
        2**17,
        "fill",
        16,
        scratch=[pltpu.VMEM((slots, 128), bf16), pltpu.SemaphoreType.DMA],
        out_specs=[HBM],
        input_output_aliases={1: 0},
    )(row, second)
    second = lax.all_to_all(second, EXPERT, split_axis=0, concat_axis=0, tiled=True)
    token_grad, router_grad, gate_grad, up_grad = call(
        combine_kernel,
        [VMEM] * 5,
        [
            ((tok_rows, features), bf16),
            ((experts, features), f32),
            ((part, hidden), bf16),
            ((part, hidden), bf16),
        ],
        2 * slots * tok_rows * features,
        2 * 2**20,
        "combine",
        16,
    )(select, zeroth, first, second, sums)
    return token_grad, gate_grad[None], up_grad[None], router_grad


def solution(mesh):
    fine = Mesh(mesh.devices.reshape(8, 2, 4, 8), DP + EXPERT)
    rows = P(DP + EXPERT, None)
    shard = P(EXPERT, DP, None)
    return jax.shard_map(
        per_device,
        mesh=fine,
        in_specs=(rows, rows, P(), shard, shard, shard, rows, P(DP + EXPERT)),
        out_specs=(rows, shard, shard, P()),
        check_vma=False,
    )
```

```python
import jax
import jax.numpy as jnp
from jax import lax
from jax.experimental import pallas as pl
from jax.experimental.pallas import tpu as pltpu
from jax.sharding import Mesh, PartitionSpec as P

f32 = jnp.float32
bf16 = jnp.bfloat16
DP = ("y", "core")
EXPERT = ("x", "z")
CHUNK = 256
WHOLE_MIB = 63
ZEROTH = 128
FIRST = 896
ROWS = (((0,), (0,)), ((), ()))
LAST = (((1,), (1,)), ((), ()))
PLAIN = (((1,), (0,)), ((), ()))


def dot(left, right, dims=PLAIN):
    return lax.dot_general(left, right, dims, preferred_element_type=f32)


def split3(value):
    high = value.astype(bf16)
    rest = value - high.astype(f32)
    mid = rest.astype(bf16)
    low = (rest - mid.astype(f32)).astype(bf16)
    return high, mid, low


def pack_shard(gate_hbm, up_hbm, down_hbm, shard, sems):
    part, hidden = gate_hbm.shape
    narrow, features = down_hbm.shape
    moves, row = [], 0
    for start in range(0, hidden, CHUNK):
        for ref in (gate_hbm, up_hbm):
            moves.append((ref.at[:, pl.ds(start, CHUNK)], shard.at[pl.ds(row, part)]))
            row += part
    for start in range(0, features, CHUNK):
        moves.append((down_hbm.at[:, pl.ds(start, CHUNK)], shard.at[pl.ds(row, narrow)]))
        row += narrow
    return [
        pltpu.make_async_copy(source, target, sems.at[i])
        for i, (source, target) in enumerate(moves)
    ]


def dispatch_kernel(
    routes_ref, mask_ref, tokens_ref, cotangent_ref, gate_hbm, up_hbm, down_hbm,
    sent_ref, select_ref, shard_hbm, tokens, cotangent, packed, select, shard, sems, shard_sems,
):
    experts, both, _ = sent_ref.shape
    capacity = both // 2
    top_count, tok_rows = routes_ref.shape
    slots = experts * capacity
    load_tokens = pltpu.make_async_copy(tokens_ref, tokens, sems.at[0])
    load_cotangent = pltpu.make_async_copy(cotangent_ref, cotangent, sems.at[1])
    load_tokens.start()
    load_cotangent.start()
    loads = pack_shard(gate_hbm, up_hbm, down_hbm, shard, shard_sems)
    for load in loads:
        load.start()
    owner = lax.broadcasted_iota(jnp.int32, (experts, tok_rows), 0)
    live = jnp.zeros((experts, tok_rows), f32)
    for k in range(top_count):
        live = live + jnp.where(routes_ref[k : k + 1, :] == owner, 1.0, 0.0)
    live = jnp.where(mask_ref[...] == 1, live, 0.0)
    row = lax.broadcasted_iota(jnp.int32, (tok_rows, tok_rows), 0)
    column = lax.broadcasted_iota(jnp.int32, (tok_rows, tok_rows), 1)
    earlier = jnp.where(row < column, 1.0, 0.0).astype(bf16)
    before = dot(live.astype(bf16), earlier)
    place = jnp.where(live > 0.5, before, -1.0).astype(bf16)
    owner = lax.broadcasted_iota(jnp.int32, (slots, experts), 0) // capacity
    spread = jnp.where(owner == lax.broadcasted_iota(jnp.int32, (slots, experts), 1), 1.0, 0.0)
    place = dot(spread.astype(bf16), place)
    index = lax.broadcasted_iota(jnp.int32, (slots, tok_rows), 0) % capacity
    select[...] = jnp.where(place == index.astype(f32), 1.0, 0.0).astype(bf16)
    stores = [pltpu.make_async_copy(select, select_ref, sems.at[2])]
    stores[0].start()
    load_tokens.wait()
    load_cotangent.wait()
    pieces = 4
    step = experts // pieces
    for piece in range(pieces):
        some = slice(piece * step, (piece + 1) * step)
        rows = select[piece * step * capacity : (piece + 1) * step * capacity, :]
        for half, ref in enumerate((tokens, cotangent)):
            packed[some, half * capacity : (half + 1) * capacity, :] = (
                dot(rows, ref[...]).astype(bf16).reshape(step, capacity, ref.shape[1])
            )
        store = pltpu.make_async_copy(packed.at[some], sent_ref.at[some], sems.at[3 + piece])
        store.start()
        stores.append(store)
        if piece == 0:
            for load in loads:
                load.wait()
            stores.append(pltpu.make_async_copy(shard, shard_hbm, sems.at[3 + pieces]))
            stores[-1].start()
    for store in stores:
        store.wait()


def expert_kernel(
    expert_ref, slots_ref, router_ref, weights_hbm,
    part_hbm, zeroth_ref, first_hbm, second_ref,
    pair_ref, down_ref, flipped_ref, part_ref, delta_ref, term_ref, first_ref, sems,
):
    sources, both, features = slots_ref.shape
    capacity = both // 2
    slots = sources * capacity
    chunks, shards, part, _ = pair_ref.shape
    part = part // 2
    hidden = chunks * CHUNK
    narrow = hidden // shards
    experts = router_ref.shape[0]
    loads = [
        pltpu.make_async_copy(
            weights_hbm.at[:, pl.ds(2 * part * i, 2 * part), :], pair_ref.at[i], sems.at[i]
        )
        for i in range(chunks)
    ]
    for i in range(features // CHUNK):
        loads.insert(
            1 + i,
            pltpu.make_async_copy(
                weights_hbm.at[:, pl.ds(2 * part * chunks + narrow * i, narrow), :],
                down_ref.at[:, :, pl.ds(i * CHUNK, CHUNK)],
                sems.at[chunks + i],
            ),
        )
    for load in loads:
        load.start()
    slot_tokens = slots_ref[:, :capacity, :].reshape(slots, features)
    slot_cotangent = slots_ref[:, capacity:, :].reshape(slots, features)
    flipped_ref[...] = slot_tokens.T

    router_high, router_mid, router_low = split3(router_ref[...])
    stack = jnp.concatenate([router_high, router_mid, router_low], axis=0)
    logits = dot(slot_tokens, stack, LAST)
    logits = logits[:, :experts] + (
        logits[:, experts : 2 * experts] + logits[:, 2 * experts :]
    )
    weights = jnp.exp(logits)
    probs = weights / jnp.sum(weights, axis=1, keepdims=True)
    mine = lax.broadcasted_iota(jnp.int32, (slots, experts), 1) == expert_ref[0]
    own = jnp.sum(jnp.where(mine, probs, 0.0), axis=1, keepdims=True)
    rounded = own.astype(bf16).astype(f32)

    prob_grad = jnp.zeros((slots, 1), f32)
    stores, todo = [], []
    for i in range(chunks):
        start = i * CHUNK
        columns = slice(start, start + CHUNK)
        if i == 0:
            loads[0].wait()
        gate = pair_ref[i, :, :part, :].reshape(features, CHUNK)
        up = pair_ref[i, :, part:, :].reshape(features, CHUNK)
        gate_proj = dot(slot_tokens, gate)
        up_proj = dot(slot_tokens, up)
        if i == 0:
            for load in loads[1:]:
                load.wait()
        pieces, row = [], start
        while row < start + CHUNK:
            shard, inside = row // narrow, row % narrow
            end = min(narrow, inside + start + CHUNK - row)
            pieces.append(down_ref[shard, inside:end, :])
            row += end - inside
        hidden_grad = dot(slot_cotangent, jnp.concatenate(pieces, axis=0), LAST)
        sigmoid_gate = 1.0 / (1.0 + jnp.exp(-gate_proj))
        activated = gate_proj * sigmoid_gate
        slope = sigmoid_gate * (1.0 + gate_proj * (1.0 - sigmoid_gate))
        prob_grad = prob_grad + jnp.sum(
            hidden_grad * activated * up_proj, axis=1, keepdims=True
        )
        scaled = rounded * hidden_grad
        gate_delta = (scaled * up_proj * slope).astype(bf16)
        up_delta = (scaled * activated).astype(bf16)
        delta_ref[0, i] = gate_delta
        delta_ref[1, i] = up_delta
        todo.append((start, gate_delta, up_delta))
    for i, (start, *pair) in enumerate(todo):
        columns = slice(start, start + CHUNK)
        for half, delta in enumerate(pair):
            product = dot(flipped_ref[...], delta).astype(bf16)
            row = (2 * i + half) * part
            part_ref[:, row : row + part, :] = product.reshape(shards, part, CHUNK)
        some = pl.ds(2 * i * part, 2 * part)
        stores.append(
            pltpu.make_async_copy(part_ref.at[:, some, :], part_hbm.at[:, some, :], sems.at[i])
        )
        stores[-1].start()
    share = prob_grad.astype(bf16).astype(f32) * own
    share = share * (jnp.where(mine, 1.0, 0.0) - probs)
    share_high, share_mid, share_low = split3(share)
    term = dot(jnp.concatenate([share_high, share_mid, share_low], axis=1), slot_tokens, ROWS)
    term = term[:experts] + (term[experts : 2 * experts] + term[2 * experts :])
    term_high, term_mid, _ = split3(term)
    for i in range(features // 128):
        columns = slice(i * 128, (i + 1) * 128)
        term_ref[:, i, :] = term_high[:, columns].astype(f32)
        term_ref[:, capacity // 2 + i, :] = term_mid[:, columns].astype(f32)
    zeroth_ref[:, ZEROTH:] = term_ref[...].astype(bf16).reshape(slots, 128)

    left = jnp.concatenate([share_high, share_high, share_mid], axis=1)
    right = jnp.concatenate([router_high, router_mid, router_high], axis=0)
    step = CHUNK // part
    blocks = features // CHUNK
    for block in [blocks - 1, *range(blocks - 1)]:
        some = slice(block * step, (block + 1) * step)
        start = block * CHUNK
        total = dot(left, right[:, start : start + CHUNK])
        for i in range(chunks):
            gate = pair_ref[i, some, :part, :].reshape(CHUNK, CHUNK)
            up = pair_ref[i, some, part:, :].reshape(CHUNK, CHUNK)
            total = total + dot(delta_ref[0, i], gate, LAST) + dot(delta_ref[1, i], up, LAST)
        total = total.astype(bf16)
        for ref, low, high in (
            (zeroth_ref, 0, ZEROTH),
            (first_ref, ZEROTH, FIRST),
            (second_ref, FIRST, features),
        ):
            begin, end = max(low, start), min(high, start + CHUNK)
            if begin < end:
                ref[:, begin - low : end - low] = total[:, begin - start : end - start]
                if ref is first_ref:
                    place = pl.ds(begin - low, end - begin)
                    stores.append(
                        pltpu.make_async_copy(
                            first_ref.at[:, place], first_hbm.at[:, place], sems.at[chunks + block]
                        )
                    )
                    stores[-1].start()
    for store in stores:
        store.wait()


def fill_kernel(row_ref, given_hbm, second_hbm, block_ref, sem):
    high, mid, _ = split3(row_ref[...])
    block = jnp.concatenate([high.astype(f32), mid.astype(f32)], axis=0).astype(bf16)
    block_ref[...] = jnp.concatenate([block] * (block_ref.shape[0] // block.shape[0]), axis=0)
    place = pl.ds(given_hbm.shape[1] - block.shape[1], block.shape[1])
    store = pltpu.make_async_copy(block_ref, second_hbm.at[:, place], sem)
    store.start()
    store.wait()


def combine_kernel(
    select_ref, zeroth_ref, first_ref, second_ref, sums_ref, out_ref, router_ref, gate_ref, up_ref
):
    experts, features = router_ref.shape
    slots = select_ref.shape[0]
    select = select_ref[...]
    rest = features - FIRST
    out_ref[:, :ZEROTH] = dot(select, zeroth_ref[:, :ZEROTH], ROWS).astype(bf16)
    out_ref[:, ZEROTH:FIRST] = dot(select, first_ref[...], ROWS).astype(bf16)
    out_ref[:, FIRST:] = dot(select, second_ref[:, :rest], ROWS).astype(bf16)
    rows = second_ref[:, rest:].astype(f32).reshape(experts, slots // experts, 128)
    half = slots // experts // 2
    rows = rows[:, :half, :] + rows[:, half:, :]
    for i in range(half):
        router_ref[:, i * 128 : (i + 1) * 128] = rows[:, i, :]
    part = gate_ref.shape[0]
    for i in range(gate_ref.shape[1] // CHUNK):
        columns = slice(i * CHUNK, (i + 1) * CHUNK)
        gate_ref[:, columns] = sums_ref[2 * i * part : (2 * i + 1) * part, :]
        up_ref[:, columns] = sums_ref[(2 * i + 1) * part : (2 * i + 2) * part, :]


def call(kernel, specs, outs, flops, size, name, mib, scratch=(), **more):
    return pl.pallas_call(
        kernel,
        out_shape=[jax.ShapeDtypeStruct(s, d) for s, d in outs],
        in_specs=specs,
        scratch_shapes=list(scratch),
        compiler_params=pltpu.CompilerParams(vmem_limit_bytes=int(mib * 2**20)),
        cost_estimate=pl.CostEstimate(flops=flops, bytes_accessed=size, transcendentals=0),
        name=name,
        **more,
    )


SMEM = pl.BlockSpec(memory_space=pltpu.SMEM)
VMEM = pl.BlockSpec(memory_space=pltpu.VMEM)
HBM = pl.BlockSpec(memory_space=pltpu.HBM)


def per_device(
    tokens, cotangent, router_weight, gate_weight, up_weight, down_weight, routes, drop_mask
):
    tok_rows, features = tokens.shape
    experts = router_weight.shape[0]
    top_count = routes.shape[1]
    _, part, hidden = gate_weight.shape
    shards = features // part
    capacity = tok_rows * top_count * 2 // (3 * experts)
    slots = experts * capacity
    chunks = hidden // CHUNK
    lines = 3 * part * chunks

    sent, select, shard = call(
        dispatch_kernel,
        [VMEM, VMEM] + [HBM] * 5,
        [
            ((experts, 2 * capacity, features), bf16),
            ((slots, tok_rows), bf16),
            ((lines, CHUNK), bf16),
        ],
        4 * slots * tok_rows * features,
        3 * 2**20,
        "dispatch",
        WHOLE_MIB,
        scratch=[
            pltpu.VMEM((tok_rows, features), bf16),
            pltpu.VMEM((tok_rows, features), bf16),
            pltpu.VMEM((experts, 2 * capacity, features), bf16),
            pltpu.VMEM((slots, tok_rows), bf16),
            pltpu.VMEM((lines, CHUNK), bf16),
            pltpu.SemaphoreType.DMA((8,)),
            pltpu.SemaphoreType.DMA((2 * chunks + features // CHUNK,)),
        ],
        out_specs=[HBM] * 3,
    )(
        routes.T,
        drop_mask.reshape(1, tok_rows),
        tokens,
        cotangent,
        gate_weight[0],
        up_weight[0],
        down_weight[0],
    )

    slot_rows = lax.all_to_all(sent, EXPERT, split_axis=0, concat_axis=0, tiled=True)
    weights = lax.all_gather(shard, DP, axis=0, tiled=True).reshape(shards, lines, CHUNK)

    expert = lax.axis_index(EXPERT).astype(jnp.int32).reshape(1)
    second_width = features - FIRST + 128
    parts, zeroth, first, second = call(
        expert_kernel,
        [SMEM, VMEM, VMEM, HBM],
        [
            ((shards, 2 * part * chunks, CHUNK), bf16),
            ((slots, ZEROTH + 128), bf16),
            ((slots, FIRST - ZEROTH), bf16),
            ((slots, second_width), bf16),
        ],
        14 * slots * features * hidden,
        10 * 2**20,
        "expert",
        48,
        scratch=[
            pltpu.VMEM((chunks, shards, 2 * part, CHUNK), bf16),
            pltpu.VMEM((shards, hidden // shards, features), bf16),
            pltpu.VMEM((features, slots), bf16),
            pltpu.VMEM((shards, 2 * part * chunks, CHUNK), bf16),
            pltpu.VMEM((2, chunks, slots, CHUNK), bf16),
            pltpu.VMEM((experts, capacity, 128), f32),
            pltpu.VMEM((slots, FIRST - ZEROTH), bf16),
            pltpu.SemaphoreType.DMA((chunks + features // CHUNK,)),
        ],
        out_specs=[HBM, VMEM, HBM, VMEM],
    )(expert, slot_rows, router_weight, weights)
    sums = lax.psum_scatter(
        parts.reshape(shards * 2 * part * chunks, CHUNK), DP, scatter_dimension=0, tiled=True
    )

    zeroth = lax.all_to_all(zeroth, EXPERT, split_axis=0, concat_axis=0, tiled=True)
    first, zeroth = lax.optimization_barrier((first, zeroth))
    first = lax.all_to_all(first, EXPERT, split_axis=0, concat_axis=0, tiled=True)
    term = zeroth.reshape(experts, capacity, -1)[:, :, ZEROTH:].astype(f32)
    term = jnp.sum(term.reshape(experts, 2, capacity // 2, 128), axis=(0, 1))
    row = jnp.sum(lax.all_gather(term, DP, axis=0), axis=0)
    row, first = lax.optimization_barrier((row, first))
    (second,) = call(
        fill_kernel,
        [VMEM, HBM],
        [((slots, second_width), bf16)],
        2**17,
        2**17,
        "fill",
        16,
        scratch=[pltpu.VMEM((slots, 128), bf16), pltpu.SemaphoreType.DMA],
        out_specs=[HBM],
        input_output_aliases={1: 0},
    )(row, second)
    second = lax.all_to_all(second, EXPERT, split_axis=0, concat_axis=0, tiled=True)
    token_grad, router_grad, gate_grad, up_grad = call(
        combine_kernel,
        [VMEM] * 5,
        [
            ((tok_rows, features), bf16),
            ((experts, features), f32),
            ((part, hidden), bf16),
            ((part, hidden), bf16),
        ],
        2 * slots * tok_rows * features,
        2 * 2**20,
        "combine",
        16,
    )(select, zeroth, first, second, sums)
    return token_grad, gate_grad[None], up_grad[None], router_grad


def solution(mesh):
    fine = Mesh(mesh.devices.reshape(8, 2, 4, 8), DP + EXPERT)
    rows = P(DP + EXPERT, None)
    shard = P(EXPERT, DP, None)
    return jax.shard_map(
        per_device,
        mesh=fine,
        in_specs=(rows, rows, P(), shard, shard, shard, rows, P(DP + EXPERT)),
        out_specs=(rows, shard, shard, P()),
        check_vma=False,
    )
```
